128 devices in a mesh: expert: 16 (over y, x), cuts: 8 (over z, core).
Axes of the slice: x: 4, y: 4, z: 4, core: 2. Of those that a mesh axis runs over, the one named last changes fastest.
Arguments:
- tokens: bfloat16 [16384, 7168], P(('expert', 'cuts')), may hold values from -130 to 130
- out_grad: bfloat16 [16384, 7168], P(('expert', 'cuts')), may hold values from -130 to 130
- combine: float32 [16384, 8], P(('expert', 'cuts')), may hold values from 0.1 to 1
- expert_ids: int32 [16384, 8], P(('expert', 'cuts')), may hold values from 0 to 383, all different within a row; in each aligned block of 128 rows (0 to 127, 128 to 255, ...) at most 4 rows name the same one
- expert_rank: int32 [384], replicated, may hold values from 0 to 383, each once
- gate_weight: bfloat16 [16, 7168, 2048], P('expert', None, 'cuts'), may hold values from -0.0625 to 0.0625
- up_weight: bfloat16 [16, 7168, 2048], P('expert', None, 'cuts'), may hold values from -0.0625 to 0.0625
- down_weight: bfloat16 [16, 2048, 7168], P('expert', 'cuts'), may hold values from -1 to 1
Outputs:
- updates: bfloat16 [16, 3, 7168, 2048], P('expert', None, 'cuts')
The draws below stay inside these ranges and needn't reach their ends.
Inputs may be any that keep to these rules, and one draw needn't show every extreme that they name: `expert_ids`: each row names 8 different experts; among the rows of one device no expert is named more than 4 times. `expert_rank`: A permutation; the experts of rank under 16 are the hot ones.
All inputs are finite; a program needn't handle non-finite values.
Results may differ from the reference program's by a relative error of at most 0.0058.
Values may be sent and summed in bfloat16 or wider, within the bound.
No kernel may reach another device: no remote copies, remote signals or barrier semaphores. Data moves between devices by JAX's collectives and lax.ppermute only.
A program may use at most 128 MiB of HBM per device.

```python
import math
import jax
import jax.numpy as jnp
import numpy as np
from jax import lax

D = 7168
FFN = 2048
ROUTED = 384
TOPK = 8
TOK_DEV = 128
HOT = 16
CAP = 4
TOKENS = 16384
N_EXPERT = 16
N_CUTS = 8


def feature_scales(key, rows, lift):
    first, second, third = jax.random.split(key, 3)
    column_pos = jnp.arange(D, dtype=jnp.float32) / (D - 1)
    column = jnp.sqrt(lift ** column_pos) * jnp.exp(jax.random.uniform(first, (D,)) * math.log(10.0)) / 4.0
    row_scale = jnp.exp(jax.random.uniform(second, (rows, 1)) * math.log(10.0)) / 3.0
    return (column * row_scale, third)


def draw_tokens(key, part):
    key = jax.random.fold_in(key, 11)
    scale, third = feature_scales(key, TOKENS, 3.0)
    base = jax.random.truncated_normal(third, -4.0, 4.0, (TOKENS, D))
    return (base * scale).astype(jnp.bfloat16)


def draw_out_grad(key, part):
    key = jax.random.fold_in(key, 23)
    scale, third = feature_scales(key, TOKENS, 3.0)
    base = jax.random.truncated_normal(third, -4.0, 4.0, (TOKENS, D))
    return (base * scale).astype(jnp.bfloat16)


def draw_down_weight(key, part):
    key = jax.random.fold_in(key, 37)
    first, second = jax.random.split(key, 2)
    row_scale = jnp.exp(jax.random.uniform(first, (HOT, FFN, 1)) * math.log(10.0)) / 3.9
    base = jax.random.truncated_normal(second, -4.0, 4.0, (HOT, FFN, D))
    return (base * row_scale / math.sqrt(FFN)).astype(jnp.bfloat16)


def level_of(key, shape, shards, least, largest):
    def one(dim, shards_of):
        steps = jax.random.uniform(jax.random.fold_in(jax.random.fold_in(key, 6), dim), (shards_of,), jnp.float32, least / len(shards), largest / len(shards))
        return jnp.repeat(jnp.exp(steps), shape[dim] // shards_of).reshape((-1,) + (1,) * (len(shape) - dim - 1))

    loudness = one(*shards[0])
    for cut in shards[1:]:
        loudness = loudness * one(*cut)
    return loudness


def shared_out(own_key, own, number, rows, amount, top, most, skew):
    order = jax.random.permutation(own_key, amount)
    crowded, ordinary = portions_of(amount, rows * top, most, skew, True), portions_of(amount, rows * top, most, skew, False)
    places = jnp.arange(amount)

    def named(tallies, rotation):
        used = int((tallies > 0).sum())
        fixed = max(1, used // 4)
        passed = fixed + (places - fixed + rotation * (used - fixed)) % max(1, amount - fixed)
        return jnp.zeros((amount,), jnp.int32).at[order[jnp.where(places < fixed, places, passed)]].set(jnp.asarray(tallies, jnp.int32))

    tallies = jnp.where(number % 4 == 0, named(crowded, number // 4), named(ordinary, number - number // 4 - 1))
    mixed = jax.random.permutation(jax.random.fold_in(own, 3), amount)
    donor, sink = mixed[0:amount // 2 * 2:2], mixed[1:amount // 2 * 2:2]
    room = jnp.minimum(tallies[donor] - 1, most - tallies[sink]) // 2
    room = jnp.where((donor == order[0]) | (sink == order[0]) | (tallies[sink] == 0), 0, jnp.maximum(room, 0))
    passed = jax.random.randint(jax.random.fold_in(own, 4), (amount // 2,), 0, 1 << 20) % (room + 1)
    tallies = tallies.at[donor].add(-passed).at[sink].add(passed)
    members = jnp.searchsorted(jnp.cumsum(tallies), jnp.arange(rows * top), side="right").astype(jnp.int32)
    table = members.reshape(top, rows).T
    table = table[jax.random.permutation(jax.random.fold_in(own, 1), rows)]
    rotation = jax.random.randint(jax.random.fold_in(own, 2), (rows, 1), 0, top)
    return jnp.take_along_axis(table, (jnp.arange(top)[None, :] + rotation) % top, axis=1)


def portions_of(amount, total, limit, lean, full):
    portions = [(1 << 20) // math.isqrt(standing ** lean) + 1 for standing in range(1, amount + 1)]
    largest = limit if full else min(limit, max(-(-total // amount), total * portions[0] // sum(portions)))
    least = 1 if total - largest >= amount - 1 else 0
    given, spare = [largest] + [least] * (amount - 1), total - largest - least * (amount - 1)
    while spare > 0:
        candidates = [i for i in range(1, amount) if given[i] < largest] or [i for i in range(1, amount) if given[i] < limit]
        pool, remaining = sum([portions[i] for i in candidates]), spare
        for i in candidates:
            addition = min(limit - given[i], max(1, remaining * portions[i] // pool), spare)
            given[i] = given[i] + addition
            spare = spare - addition
    return np.array(given)


def normal_values(rng, extent, deviation, bound, cuts=(), kind=jnp.bfloat16):
    factor_of = level_of(rng, extent, cuts, -0.22, 0.18) if cuts else 1.0
    values = jax.random.normal(rng, extent, jnp.float32) * deviation * factor_of
    return jnp.minimum(jnp.maximum(values, -bound), bound).astype(kind)


def setup_inputs(seed: int = 0) -> dict:
    splits = jax.random.split(jax.random.key(seed), 9)
    tokens = draw_tokens(jax.random.fold_in(splits[8], 71), 0)
    out_grad = draw_out_grad(jax.random.fold_in(splits[8], 71), 0)
    combine = jnp.clip(0.1 + 0.9 * jax.random.uniform(splits[2], (TOKENS, TOPK), jnp.float32) ** level_of(splits[2], (TOKENS, TOPK), ((0, 128),), -0.2, 0.2), 0.1, 1.0)
    expert_ids_keys = jax.random.split(jax.random.fold_in(splits[3], 1), TOKENS // TOK_DEV)
    expert_ids_turns = jax.random.permutation(jax.random.fold_in(splits[3], 3), TOKENS // TOK_DEV)
    expert_ids = jax.vmap(lambda own, number: shared_out(jax.random.fold_in(splits[3], 2), own, number, TOK_DEV, ROUTED, TOPK, CAP, 2))(expert_ids_keys, expert_ids_turns).reshape((TOKENS, TOPK))
    expert_rank = jax.random.permutation(splits[4], ROUTED).astype(jnp.int32)
    gate_weight = normal_values(splits[5], (HOT, D, FFN), D ** -0.5, 0.0625, ((0, 16), (2, 8)))
    up_weight = normal_values(splits[6], (HOT, D, FFN), D ** -0.5, 0.0625, ((0, 16), (2, 8)))
    down_weight = draw_down_weight(jax.random.fold_in(splits[8], 71), 0)
    return {"tokens": tokens, "out_grad": out_grad, "combine": combine, "expert_ids": expert_ids, "expert_rank": expert_rank, "gate_weight": gate_weight, "up_weight": up_weight, "down_weight": down_weight}


EPSILON = 1e-06

def dispatch_rows(tokens, out_grad, combine, expert_ids, expert_rank, hot_count, capacity):
    tok_count = expert_ids.shape[0]
    routed = expert_rank.shape[0]
    id_match = (expert_ids[:, :, None] == jnp.arange(routed, dtype=jnp.int32)).astype(jnp.int32)
    rank_of = lax.optimization_barrier(jnp.sum(id_match * expert_rank, axis=2))
    hot_hits = (rank_of[:, :, None] == jnp.arange(hot_count, dtype=jnp.int32)).astype(jnp.int32)
    flat_hits = hot_hits.reshape(-1, hot_count)
    before = jnp.cumsum(flat_hits, axis=0) - flat_hits
    slot_index = lax.optimization_barrier(jnp.sum(before * flat_hits, axis=1)).reshape(tok_count, -1)
    placed = (slot_index[:, :, None] == jnp.arange(capacity, dtype=jnp.int32)).astype(jnp.float32)
    hot_float = hot_hits.astype(jnp.float32)
    select = jnp.einsum('tkh,tkc->hct', hot_float, placed)
    scaled = jnp.einsum('tkh,tkc,tk->hct', hot_float, placed, combine, precision=lax.Precision.HIGHEST)
    width = tokens.shape[1]
    tok_rows = jnp.dot(select.reshape(hot_count * capacity, tok_count).astype(jnp.bfloat16), tokens, preferred_element_type=jnp.float32).astype(jnp.bfloat16)
    grad_rows = jnp.dot(scaled.reshape(hot_count * capacity, tok_count), out_grad.astype(jnp.float32), precision=lax.Precision.HIGHEST).astype(jnp.bfloat16)
    return (tok_rows.reshape(hot_count, capacity, width), grad_rows.reshape(hot_count, capacity, width))

def expert_grads(x_rows, g_rows, w_gate, w_up, w_down):
    gate_act = jnp.dot(x_rows, w_gate, preferred_element_type=jnp.float32)
    up_act = jnp.dot(x_rows, w_up, preferred_element_type=jnp.float32)
    sigmoid_gate = jax.nn.sigmoid(gate_act)
    hidden = (gate_act * sigmoid_gate * up_act).astype(jnp.bfloat16)
    act_grad = lax.dot_general(g_rows, w_down, (((1,), (1,)), ((), ())), preferred_element_type=jnp.float32)
    gate_grad = (act_grad * up_act * sigmoid_gate * (1.0 + gate_act * (1.0 - sigmoid_gate))).astype(jnp.bfloat16)
    up_grad = (act_grad * gate_act * sigmoid_gate).astype(jnp.bfloat16)
    row_dims = (((0,), (0,)), ((), ()))
    return jnp.stack([lax.dot_general(x_rows, gate_grad, row_dims, preferred_element_type=jnp.float32), lax.dot_general(x_rows, up_grad, row_dims, preferred_element_type=jnp.float32), lax.dot_general(g_rows, hidden, row_dims, preferred_element_type=jnp.float32)])

def reference(tokens, out_grad, combine, expert_ids, expert_rank, gate_weight, up_weight, down_weight):
    devices = N_EXPERT * N_CUTS

    def per_device(pieces):
        return dispatch_rows(pieces[0], pieces[1], pieces[2], pieces[3], expert_rank, HOT, CAP)
    tok_bufs, grad_bufs = lax.map(per_device, (tokens.reshape(devices, TOK_DEV, D), out_grad.reshape(devices, TOK_DEV, D), combine.reshape(devices, TOK_DEV, TOPK), expert_ids.reshape(devices, TOK_DEV, TOPK)))
    tok_bufs = jnp.transpose(tok_bufs, (1, 0, 2, 3)).reshape(HOT, devices * CAP, D)
    grad_bufs = jnp.transpose(grad_bufs, (1, 0, 2, 3)).reshape(HOT, devices * CAP, D)

    def per_expert(pieces):
        gradients = expert_grads(pieces[0], pieces[1], pieces[2], pieces[3], pieces[4])
        total = lax.optimization_barrier(jnp.sum(gradients * gradients, axis=(1, 2)))
        factor = lax.rsqrt(total / (D * FFN) + EPSILON)
        return (gradients * factor[:, None, None]).astype(jnp.bfloat16)
    return lax.map(per_expert, (tok_bufs, grad_bufs, gate_weight, up_weight, down_weight))
```

```python
import functools

import jax
import jax.numpy as jnp
from jax import lax
from jax.experimental import pallas as pl
from jax.experimental.pallas import tpu as pltpu
from jax.sharding import Mesh
from jax.sharding import PartitionSpec as P

CAP = 4
EPSILON = 1e-06
TILE = 896
F32 = jnp.float32
BF16 = jnp.bfloat16
ANY = pl.BlockSpec(memory_space=pl.ANY)
VMEM = pl.BlockSpec(memory_space=pltpu.VMEM)
SMEM = pl.BlockSpec(memory_space=pltpu.SMEM)


def params(mib):
    return pltpu.CompilerParams(vmem_limit_bytes=mib * 1024 * 1024)


def iota(shape, dim):
    return lax.broadcasted_iota(jnp.int32, shape, dim)


def dispatch_kernel(ids_ref, comb_ref, rank_ref, tok_ref, grad_ref, out_ref, sel_ref, scale_ref):
    rows = out_ref.shape[0]
    toks = tok_ref.shape[0]

    @pl.when(pl.program_id(0) == 0)
    def _():
        ranks = rank_ref[...]
        routed = ranks.shape[1]
        expert_row = iota((rows, routed), 0) // (2 * CAP)
        ident = jnp.sum(
            jnp.where(ranks == expert_row, iota((rows, routed), 1), 0), axis=1, keepdims=True
        )
        hit = jnp.zeros((rows, toks), F32)
        comb = jnp.zeros((rows, toks), F32)
        for k in range(ids_ref.shape[0]):
            same = ids_ref[k : k + 1, :] == ident
            hit = jnp.where(same, 1.0, hit)
            comb = jnp.where(same, comb_ref[k : k + 1, :], comb)
        earlier = (iota((toks, toks), 0) < iota((toks, toks), 1)).astype(BF16)
        slot = jnp.dot(hit.astype(BF16), earlier, preferred_element_type=F32)
        row = iota((rows, toks), 0)
        want = (row % CAP).astype(F32)
        is_grad = (row // CAP) % 2 == 1
        sel = jnp.where(slot == want, hit, 0.0)
        sel_ref[:, :toks] = jnp.where(is_grad, 0.0, sel).astype(BF16)
        sel_ref[:, toks:] = jnp.where(is_grad, sel, 0.0).astype(BF16)
        weight = jnp.sum(sel * comb, axis=1, keepdims=True)
        scale_ref[...] = jnp.where(is_grad, weight, 1.0)

    both = jnp.concatenate([tok_ref[...], grad_ref[...]], axis=0)
    picked = jnp.dot(sel_ref[...], both, preferred_element_type=F32)
    out_ref[...] = (picked * scale_ref[:, :1]).astype(BF16)


def dispatch(ids, comb, ranks, tokens, out_grad, first, tiles, rows):
    toks = tokens.shape[0]
    whole = lambda j: (0, 0)
    piece = lambda j: (0, j + first)
    return pl.pallas_call(
        dispatch_kernel,
        grid=(tiles,),
        in_specs=[
            pl.BlockSpec(ids.shape, whole),
            pl.BlockSpec(comb.shape, whole),
            pl.BlockSpec(ranks.shape, whole),
            pl.BlockSpec((toks, TILE), piece),
            pl.BlockSpec((toks, TILE), piece),
        ],
        out_specs=pl.BlockSpec((rows, TILE), lambda j: (0, j)),
        out_shape=jax.ShapeDtypeStruct((rows, tiles * TILE), BF16),
        scratch_shapes=[pltpu.VMEM((rows, 2 * toks), BF16), pltpu.VMEM((rows, toks), F32)],
        compiler_params=params(16),
        name="dispatch",
    )(ids, comb, ranks, tokens, out_grad)


def split_kernel(in_ref, out_ref):
    rows = in_ref.shape[0]
    half = rows // 2
    r, c = iota((rows, rows), 0), iota((rows, rows), 1)
    group = r % half
    source = (group // CAP) * (2 * CAP) + (r // half) * CAP + group % CAP
    perm = (c == source).astype(BF16)
    out_ref[...] = jnp.dot(perm, in_ref[...], preferred_element_type=F32).astype(BF16)


def split_rows(block):
    rows, width = block.shape
    spec = pl.BlockSpec((rows, TILE), lambda j: (0, j))
    return pl.pallas_call(
        split_kernel,
        grid=(width // TILE,),
        in_specs=[spec],
        out_specs=spec,
        out_shape=jax.ShapeDtypeStruct(block.shape, BF16),
        compiler_params=params(16),
        name="split_rows",
    )(block)


def shift(n, k):
    return [(i, (i + k) % n) for i in range(n)]


def gather_z(block, half):
    up = lax.ppermute(block, "z", shift(4, 1))
    down = lax.ppermute(block, "z", shift(4, 3))
    far_a = lax.ppermute(up[:half], "z", shift(4, 1))
    far_b = lax.ppermute(down[half:], "z", shift(4, 3))
    return [block, up, down, far_a, far_b]


def gather_cuts(block, half):
    mine = gather_z(block, half)
    other = [lax.ppermute(t, "core", shift(2, 1)) for t in mine]
    return mine + other


def canon_blocks():
    z, c = lax.axis_index("z"), lax.axis_index("core")
    out = []
    for core in (c, 1 - c):
        for dz in (0, 3, 1, 2):
            out.append(((z + dz) % 4) * 2 + core)
    return jnp.stack(out).astype(jnp.int32)


def fetch_rows(order_ref, blocks, x_s, g_s, column, width, x_sem, g_sem):
    span = pl.ds(column, width)
    n = x_s.shape[0] // 8
    for i in range(8):
        own, up, down, far_a, far_b = blocks[5 * (i // 4) : 5 * (i // 4) + 5]
        at = pl.ds(pl.multiple_of(order_ref[i] * n, n), n)
        kind = i % 4
        if kind < 3:
            ref = (own, up, down)[kind]
            xs, gs = ref.at[pl.ds(0, n), span], ref.at[pl.ds(n, n), span]
        else:
            xs, gs = far_a.at[:, span], far_b.at[:, span]
        pltpu.make_async_copy(xs, x_s.at[at, :], x_sem).start()
        pltpu.make_async_copy(gs, g_s.at[at, :], g_sem).start()


def act_dots(x_s, g_s, wg_s, wu_s, wd_s, gate, up, act):
    gate[...] += jnp.dot(x_s[...], wg_s[...], preferred_element_type=F32)
    up[...] += jnp.dot(x_s[...], wu_s[...], preferred_element_type=F32)
    act[...] += lax.dot_general(
        g_s[...], wd_s[...], (((1,), (1,)), ((), ())), preferred_element_type=F32
    )


def acts_kernel(first, tiles, last, order_ref, *refs):
    blocks = refs[:10]
    wg, wu, wd = refs[10:13]
    refs = refs[13:]
    if last:
        before, out_ref = refs[0], refs[1]
        x_s, g_s, wg_s, wu_s, wd_s, acc, sems = refs[2:]
    else:
        acc = refs[0]
        x_s, g_s, wg_s, wu_s, wd_s, sems = refs[1:]
    for j in range(tiles):
        rows = pl.ds((first + j) * TILE, TILE)
        fetch_rows(
            order_ref, blocks, x_s.at[j], g_s.at[j], j * TILE, TILE, sems.at[0, j], sems.at[1, j]
        )
        pltpu.make_async_copy(wg.at[rows, :], wg_s.at[j], sems.at[2, j]).start()
        pltpu.make_async_copy(wu.at[rows, :], wu_s.at[j], sems.at[3, j]).start()
        pltpu.make_async_copy(wd.at[:, rows], wd_s.at[j], sems.at[4, j]).start()
    if last:
        acc[...] = before[...]
    else:
        acc[...] = jnp.zeros_like(acc)

    @pl.loop(0, tiles)
    def _(j):
        for k, ref in enumerate((x_s, g_s, wg_s, wu_s, wd_s)):
            pltpu.make_async_copy(ref.at[j], ref.at[j], sems.at[k, j]).wait()
        act_dots(
            x_s.at[j], g_s.at[j], wg_s.at[j], wu_s.at[j], wd_s.at[j],
            acc.at[0], acc.at[1], acc.at[2],
        )

    if last:
        n = acc.shape[2]
        step = 64

        @pl.loop(0, acc.shape[1] // step)
        def _(i):
            at = pl.ds(i * step, step)
            gate, up, act = acc[0, at, :], acc[1, at, :], acc[2, at, :]
            sig = jax.nn.sigmoid(gate)
            out_ref[at, 0:n] = (act * up * sig * (1.0 + gate * (1.0 - sig))).astype(BF16)
            out_ref[at, n : 2 * n] = (act * gate * sig).astype(BF16)
            out_ref[at, 2 * n : 3 * n] = (gate * sig * up).astype(BF16)


def acts(order, blocks, wg, wu, wd, first, before):
    n = wg.shape[1]
    tiles = blocks[0].shape[1] // TILE
    rows = 4 * blocks[0].shape[0]
    last = before is not None
    scratch = [
        pltpu.VMEM((tiles, rows, TILE), BF16),
        pltpu.VMEM((tiles, rows, TILE), BF16),
        pltpu.VMEM((tiles, TILE, n), BF16),
        pltpu.VMEM((tiles, TILE, n), BF16),
        pltpu.VMEM((tiles, n, TILE), BF16),
    ]
    if last:
        scratch.append(pltpu.VMEM((3, rows, n), F32))
        out = jax.ShapeDtypeStruct((rows, 3 * n), BF16)
    else:
        out = jax.ShapeDtypeStruct((3, rows, n), F32)
    scratch.append(pltpu.SemaphoreType.DMA((5, tiles)))
    return pl.pallas_call(
        functools.partial(acts_kernel, first, tiles, last),
        in_specs=[SMEM] + [ANY] * 13 + ([VMEM] if last else []),
        out_specs=VMEM,
        out_shape=out,
        scratch_shapes=scratch,
        compiler_params=params(40),
        cost_estimate=pl.CostEstimate(
            flops=6 * rows * tiles * TILE * n,
            bytes_accessed=4 * rows * tiles * TILE + 6 * n * tiles * TILE,
            transcendentals=0,
        ),
        name="acts",
    )(order, *blocks, wg, wu, wd, *([before] if last else []))


def squares_kernel(tiles_a, tiles, order_ref, *refs):
    blocks_a, blocks_b, hid = refs[:10], refs[10:20], refs[20]
    sums_ref, xt_ref, gt_ref = refs[21:24]
    x_s, g_s, hid_t, parts, sems = refs[24:]
    for j in range(tiles):
        blocks, column = (blocks_a, j) if j < tiles_a else (blocks_b, j - tiles_a)
        fetch_rows(
            order_ref, blocks, x_s.at[j], g_s.at[j], column * TILE, TILE, sems.at[0, j], sems.at[1, j]
        )
    n = hid.shape[1] // 3
    hid_t[...] = hid[...].T
    parts[...] = jnp.zeros_like(parts)

    @pl.loop(0, tiles)
    def _(j):
        for k, ref in enumerate((x_s, g_s)):
            pltpu.make_async_copy(ref.at[j], ref.at[j], sems.at[k, j]).wait()

        @pl.when(j == order_ref[0])
        def _():
            xt_ref[...] = x_s[j].T
            gt_ref[...] = g_s[j].T

        for m in range(3):
            src = g_s if m == 2 else x_s
            for h in range(0, n, 128):
                grads = jnp.dot(
                    hid_t[m * n + h : m * n + h + 128, :], src[j], preferred_element_type=F32
                )
                sq = grads * grads
                parts[m] += jnp.sum(sq.reshape(16, 8, TILE), axis=0)

    row = iota((8, 128), 0)
    result = jnp.zeros((8, 128), F32)
    for m in range(3):
        result = jnp.where(row == m, jnp.sum(parts[m]), result)
    sums_ref[...] = result


def squares(order, blocks_a, blocks_b, hid):
    tiles_a = blocks_a[0].shape[1] // TILE
    tiles = tiles_a + blocks_b[0].shape[1] // TILE
    rows = hid.shape[0]
    return pl.pallas_call(
        functools.partial(squares_kernel, tiles_a, tiles),
        in_specs=[SMEM] + [ANY] * 20 + [VMEM],
        out_specs=(VMEM, VMEM, VMEM),
        out_shape=(
            jax.ShapeDtypeStruct((8, 128), F32),
            jax.ShapeDtypeStruct((TILE, rows), BF16),
            jax.ShapeDtypeStruct((TILE, rows), BF16),
        ),
        scratch_shapes=[
            pltpu.VMEM((tiles, rows, TILE), BF16),
            pltpu.VMEM((tiles, rows, TILE), BF16),
            pltpu.VMEM((hid.shape[1], rows), BF16),
            pltpu.VMEM((3, 8, TILE), F32),
            pltpu.SemaphoreType.DMA((2, tiles)),
        ],
        compiler_params=params(32),
        cost_estimate=pl.CostEstimate(
            flops=2 * rows * tiles * TILE * hid.shape[1],
            bytes_accessed=4 * rows * tiles * TILE,
            transcendentals=0,
        ),
        name="squares",
    )(order, *blocks_a, *blocks_b, hid)


def final_kernel(entries, order_ref, *refs):
    blocks = refs[:10]
    xt_ref, gt_ref, total_ref, out_ref, hid, stage, in_sems, out_sems = refs[10:]
    half = hid.shape[1] // 2
    for i in range(8):
        own = blocks[5 * (i // 4) : 5 * (i // 4) + 5]
        kind = i % 4
        if kind < 3:
            pltpu.make_async_copy(own[kind], hid.at[i], in_sems.at[i]).start()
        else:
            pltpu.make_async_copy(own[3], hid.at[i, pl.ds(0, half), :], in_sems.at[i]).start()
            pltpu.make_async_copy(own[4], hid.at[i, pl.ds(half, half), :], in_sems.at[i]).start()
    n = hid.shape[2] // 3
    factors = [lax.rsqrt(total_ref[m : m + 1, 0:1] / entries + EPSILON) for m in range(3)]

    def store(slot, i):
        at = pl.ds(pl.multiple_of(order_ref[i] * n, n), n)
        return pltpu.make_async_copy(stage.at[slot], out_ref.at[:, :, at], out_sems.at[slot])

    @pl.loop(0, 8)
    def _(i):
        slot = i % 2
        pltpu.make_async_copy(hid.at[i], hid.at[i], in_sems.at[i]).wait()

        @pl.when(i >= 2)
        def _():
            store(slot, i - 2).wait()

        for m in range(3):
            lhs = gt_ref if m == 2 else xt_ref
            grads = jnp.dot(
                lhs[...], hid[i, :, m * n : (m + 1) * n], preferred_element_type=F32
            )
            stage[slot, m] = (grads * factors[m]).astype(BF16)
        store(slot, i).start()

    store(0, 6).wait()
    store(1, 7).wait()


def final(order, hid_blocks, xt, gt, total, entries):
    rows, width = hid_blocks[0].shape
    n = width // 3
    return pl.pallas_call(
        functools.partial(final_kernel, entries),
        in_specs=[SMEM] + [ANY] * 10 + [VMEM] * 3,
        out_specs=ANY,
        out_shape=jax.ShapeDtypeStruct((3, TILE, 8 * n), BF16),
        scratch_shapes=[
            pltpu.VMEM((8, rows, width), BF16),
            pltpu.VMEM((2, 3, TILE, n), BF16),
            pltpu.SemaphoreType.DMA((8,)),
            pltpu.SemaphoreType.DMA((2,)),
        ],
        compiler_params=params(32),
        name="final",
    )(order, *hid_blocks, xt, gt, total)


def body(tokens, out_grad, combine, expert_ids, expert_rank, gate_weight, up_weight, down_weight):
    width = tokens.shape[1]
    hot = lax.axis_size(("y", "x"))
    rows = hot * 2 * CAP
    ids, comb, ranks = expert_ids.T, combine.T, expert_rank[None]
    wg, wu, wd = gate_weight[0], up_weight[0], down_weight[0]
    order = canon_blocks()
    tiles = width // TILE
    split = 3
    gathered = []
    for first, count in ((0, split), (split, tiles - split)):
        sent = dispatch(ids, comb, ranks, tokens, out_grad, first, count, rows)
        sent = sent.reshape(hot, 2 * CAP, count * TILE)
        got = lax.all_to_all(sent, ("y", "x"), split_axis=0, concat_axis=0, tiled=True)
        block = split_rows(got.reshape(rows, count * TILE))
        gathered.append(gather_cuts(block, rows // 2))
    part = acts(order, gathered[0], wg, wu, wd, 0, None)
    hid = acts(order, gathered[1], wg, wu, wd, split, part)
    hid_blocks = gather_cuts(hid, hid.shape[0] // 2)
    sums, xt, gt = squares(order, gathered[0], gathered[1], hid)
    total = lax.psum(sums, ("z", "core"))
    entries = width * wg.shape[1] * 8
    return final(order, hid_blocks, xt, gt, total, entries)[None]


def solution(mesh):
    fine = Mesh(mesh.devices.reshape(4, 4, 4, 2), ("y", "x", "z", "core"))
    expert, cuts = ("y", "x"), ("z", "core")
    tokens = P(expert + cuts, None)
    return jax.shard_map(
        body,
        mesh=fine,
        in_specs=(
            tokens,
            tokens,
            tokens,
            tokens,
            P(),
            P(expert, None, cuts),
            P(expert, None, cuts),
            P(expert, cuts, None),
        ),
        out_specs=P(expert, None, cuts, None),
        check_vma=False,
    )
```

```python
import functools

import jax
import jax.numpy as jnp
from jax import lax
from jax.experimental import pallas as pl
from jax.experimental.pallas import tpu as pltpu
from jax.sharding import Mesh
from jax.sharding import PartitionSpec as P

CAP = 4
ROW_BITS = 3
EPSILON = 1e-06
TILE = 896
AHEAD = 3
EARLY = 2
F32 = jnp.float32
BF16 = jnp.bfloat16
ANY = pl.BlockSpec(memory_space=pl.ANY)
HBM = pl.BlockSpec(memory_space=pltpu.HBM)
VMEM = pl.BlockSpec(memory_space=pltpu.VMEM)


def params(mib):
    return pltpu.CompilerParams(vmem_limit_bytes=mib * 1024 * 1024)


NEAR_Z = (0, 3, 1)


def in_hbm(*arrays):
    return [pltpu.with_memory_space_constraint(t, pltpu.HBM) for t in arrays]


def in_vmem(*shapes):
    return tuple(pltpu.VMEM(shape, dtype) for shape, dtype in shapes)


def iota(shape, dim):
    return lax.broadcasted_iota(jnp.int32, shape, dim)


def dispatch_kernel(first, tiles, ids_ref, comb_ref, rank_ref, tok, grad, out_ref, both, sems):
    rows = out_ref.shape[0]
    toks = tok.shape[0]
    for j in range(tiles):
        span = pl.ds((first + j) * TILE, TILE)
        pltpu.make_async_copy(tok.at[:, span], both.at[j, pl.ds(0, toks), :], sems.at[j]).start()
        pltpu.make_async_copy(grad.at[:, span], both.at[j, pl.ds(toks, toks), :], sems.at[j]).start()
    routed = rank_ref.shape[0]
    ranks = rank_ref[...].reshape(1, routed)
    expert_row = iota((rows, routed), 0) >> ROW_BITS
    ident = jnp.sum(
        jnp.where(ranks == expert_row, iota((rows, routed), 1), 0), axis=1, keepdims=True
    )
    hit = jnp.zeros((rows, toks), F32)
    comb = jnp.zeros((rows, toks), F32)
    for k in range(ids_ref.shape[0]):
        same = ids_ref[k : k + 1, :] == ident
        hit = jnp.where(same, 1.0, hit)
        comb = jnp.where(same, comb_ref[k : k + 1, :], comb)
    earlier = (iota((toks, toks), 0) < iota((toks, toks), 1)).astype(BF16)
    slot = jnp.dot(hit.astype(BF16), earlier, preferred_element_type=F32)
    row = iota((rows, toks), 0)
    want = (row & (CAP - 1)).astype(F32)
    is_grad = (row & CAP) != 0
    sel = jnp.where(slot == want, hit, 0.0)
    select = jnp.concatenate(
        [jnp.where(is_grad, 0.0, sel), jnp.where(is_grad, sel, 0.0)], axis=1
    ).astype(BF16)
    weight = jnp.sum(sel * comb, axis=1, keepdims=True)
    scale = jnp.where(is_grad[:, :1], weight, 1.0)
    for j in range(tiles):
        pltpu.make_async_copy(both.at[j], both.at[j], sems.at[j]).wait()
        picked = jnp.dot(select, both[j], preferred_element_type=F32)
        out_ref[:, j * TILE : (j + 1) * TILE] = (picked * scale).astype(BF16)


def dispatch(ids, comb, ranks, tokens, out_grad, first, tiles, rows):
    toks = tokens.shape[0]
    return pl.pallas_call(
        functools.partial(dispatch_kernel, first, tiles),
        in_specs=[VMEM, VMEM, VMEM, HBM, HBM],
        out_specs=VMEM,
        out_shape=jax.ShapeDtypeStruct((rows, tiles * TILE), BF16),
        scratch_shapes=[
            pltpu.VMEM((tiles, 2 * toks, TILE), BF16),
            pltpu.SemaphoreType.DMA((tiles,)),
        ],
        compiler_params=params(20),
        cost_estimate=pl.CostEstimate(
            flops=tiles * 8 * toks * rows * TILE, bytes_accessed=tiles * 6 * toks * TILE, transcendentals=0
        ),
        name="dispatch",
    )(ids, comb, ranks, *in_hbm(tokens, out_grad))


def split_kernel(order, in_ref, out_ref):
    source_count, width = in_ref.shape[0], in_ref.shape[2]
    rows = source_count * 2 * CAP
    half = rows // 2
    r, c = iota((rows, rows), 0), iota((rows, rows), 1)
    group = r & (half - 1)
    source = (group & -CAP) * 2 + jnp.where(r >= half, CAP, 0) + (group & (CAP - 1))
    perm = (c == source).astype(BF16)
    for i, place in enumerate(order):
        block = in_ref[:, i * 2 * CAP : (i + 1) * 2 * CAP, :].reshape(rows, width)
        out_ref[place * rows : (place + 1) * rows, :] = jnp.dot(
            perm, block, preferred_element_type=F32
        ).astype(BF16)


def split_rows(block, order):
    rows = block.shape[0] * block.shape[1]
    return pl.pallas_call(
        functools.partial(split_kernel, order),
        in_specs=[VMEM],
        out_specs=VMEM,
        out_shape=jax.ShapeDtypeStruct((rows, block.shape[2]), BF16),
        compiler_params=params(16),
        name="split_rows",
    )(block)


def shift(n, k):
    return [(i, (i + k) % n) for i in range(n)]


def along(x, k):
    return lax.ppermute(x, "z", shift(4, k))


def swap(x):
    return lax.ppermute(x, "core", shift(2, 1))


def after(x, dep):
    return lax.optimization_barrier((x, dep))[0]


def near_z(block):
    return [block, along(block, 1), along(block, 3)]


def far_z(up, down, half):
    return [along(up[:half], 1), along(down[half:], 3)]


def with_other(mine):
    return list(mine) + [swap(t) for t in mine]


def position(dc, dz):
    z = lax.rem(lax.axis_index("z") + dz, 4)
    return z * 2 + lax.rem(lax.axis_index("core") + dc, 2)


class Rows:
    def __init__(self, first, arrays, kind, groups):
        self.first, self.arrays, self.kind, self.groups = first, arrays, kind, groups
        self.width = arrays[0].shape[1]

    def sources(self, refs, a, n):
        refs = refs[a * len(refs) // 2 : (a + 1) * len(refs) // 2]
        out = []
        for group in self.groups:
            if self.kind == "whole":
                out.append((group, refs[0], 2 * n * group, refs[0], 2 * n * group + n))
            elif group < 3:
                ref = refs[(1, 0, 2)[group]]
                out.append((group, ref, 0, ref, n))
            else:
                out.append((group, refs[-2], 0, refs[-1], 0))
        return out

    def start(self, refs, x_s, g_s, column, width, x_sem, g_sem):
        span = pl.ds(column, width)
        n = x_s.shape[0] // (2 * len(self.groups))
        core = lax.axis_index("core")
        for a in range(2):
            here = core if a == 0 else 1 - core
            for group, x, x_row, g, g_row in self.sources(refs, a, n):
                at = pl.multiple_of((group - self.groups[0]) * 2 * n + here * n, n)
                at = pl.ds(at, n)
                pltpu.make_async_copy(x.at[pl.ds(x_row, n), span], x_s.at[at, :], x_sem).start()
                pltpu.make_async_copy(g.at[pl.ds(g_row, n), span], g_s.at[at, :], g_sem).start()


def acts_kernel(rows_of, skip, last, keep, given, *refs):
    blocks, refs = refs[: len(rows_of.arrays)], refs[len(rows_of.arrays) :]
    weights, refs = refs[:3], refs[3:]
    if skip is not None:
        before, refs = refs[0], refs[1:]
    out_ref, x_s, g_s = refs[:3]
    refs = refs[3:]
    if given:
        held = weights
    else:
        held, refs = refs[:3], refs[3:]
    sems, acc_sem = refs[:2]
    acc = refs[2] if last else out_ref
    rows = acc.shape[1]
    count = rows_of.width // TILE
    if skip is not None:
        pltpu.make_async_copy(before.at[:, pl.ds(skip, rows), :], acc, acc_sem).start()

    def views(j):
        span = pl.ds(j * TILE, TILE)
        return (
            x_s.at[:, span], g_s.at[:, span], held[0].at[span, :], held[1].at[span, :], held[2].at[:, span]
        )

    def start(j):
        x, g, wg, wu, wd = views(j)
        span = pl.ds(rows_of.first + j * TILE, TILE)
        if not given:
            pltpu.make_async_copy(weights[0].at[span, :], wg, sems.at[2, j]).start()
            pltpu.make_async_copy(weights[1].at[span, :], wu, sems.at[3, j]).start()
        rows_of.start(blocks, x, g, j * TILE, TILE, sems.at[0, j], sems.at[1, j])
        if not given:
            pltpu.make_async_copy(weights[2].at[:, span], wd, sems.at[4, j]).start()

    for j in range(min(AHEAD, count)):
        start(j)
    if skip is not None:
        pltpu.make_async_copy(acc, acc, acc_sem).wait()
    for j in range(count):
        x, g, wg, wu, wd = views(j)
        for k, ref in enumerate((x, g) if given else (x, g, wg, wu, wd)):
            pltpu.make_async_copy(ref, ref, sems.at[k, j]).wait()
        if j + AHEAD < count:
            start(j + AHEAD)
        new = (
            jnp.dot(x[...], wg[...], preferred_element_type=F32),
            jnp.dot(x[...], wu[...], preferred_element_type=F32),
            lax.dot_general(
                g[...], wd[...], (((1,), (1,)), ((), ())), preferred_element_type=F32
            ),
        )
        for k in range(3):
            if j == 0 and skip is None:
                acc[k] = new[k]
            else:
                acc[k] += new[k]

    if last:
        m = acc.shape[2]
        step = 64

        @pl.loop(0, rows // step)
        def _(i):
            at = pl.ds(pl.multiple_of(i * step, step), step)
            gate, up, act = acc[0, at, :], acc[1, at, :], acc[2, at, :]
            sig = jax.nn.sigmoid(gate)
            out_ref[at, 0:m] = (act * up * sig * (1.0 + gate * (1.0 - sig))).astype(BF16)
            out_ref[at, m : 2 * m] = (act * gate * sig).astype(BF16)
            out_ref[at, 2 * m : 3 * m] = (gate * sig * up).astype(BF16)


def acts(rows_of, n, weights, last, mib, before=None, skip=None, keep=False, given=False):
    m = weights[2].shape[0]
    rows = 2 * n * len(rows_of.groups)
    width = rows_of.width
    out = ((rows, 3 * m), BF16) if last else ((3, rows, m), F32)
    outs = [out, ((rows, width), BF16), ((rows, width), BF16)]
    held = [((width, m), BF16), ((width, m), BF16), ((m, width), BF16)]
    scratch = []
    if keep:
        outs += held
    elif not given:
        scratch += [pltpu.VMEM(*shape) for shape in held]
    scratch += [pltpu.SemaphoreType.DMA((5, width // TILE)), pltpu.SemaphoreType.DMA(())]
    if last:
        scratch.append(pltpu.VMEM((3, rows, m), F32))
    extra = [] if before is None else [before]
    return pl.pallas_call(
        functools.partial(acts_kernel, rows_of, skip, last, keep, given),
        in_specs=[HBM] * len(rows_of.arrays) + [VMEM if given else HBM] * 3 + [VMEM] * len(extra),
        out_specs=(VMEM,) * len(outs),
        out_shape=in_vmem(*outs),
        scratch_shapes=scratch,
        compiler_params=params(mib),
        cost_estimate=pl.CostEstimate(
            flops=6 * rows * width * m,
            bytes_accessed=4 * rows * width + 6 * m * width,
            transcendentals=0,
        ),
        name="acts",
    )(*in_hbm(*rows_of.arrays), *(weights if given else in_hbm(*weights)), *extra)


def squares_kernel(x0, g0, xa, ga, xb, gb, hid_a, hid_b, last_ref, xt_ref, gt_ref, hid_t, parts):
    m = hid_a.shape[1] // 3
    rows_a = hid_a.shape[0]
    hid_t[:, :rows_a] = hid_a[...].T
    hid_t[:, rows_a:] = hid_b[...].T
    parts[...] = jnp.zeros_like(parts)
    mine = position(0, 0)

    def tile(j, x, g):
        @pl.when(j == mine)
        def _():
            xt_ref[...] = x.T
            gt_ref[...] = g.T

        both = jnp.dot(hid_t[: 2 * m, :], x, preferred_element_type=F32)
        down = jnp.dot(hid_t[2 * m :, :], g, preferred_element_type=F32)
        for i, grads in enumerate((both[:m], both[m:], down)):
            parts[i] += jnp.sum((grads * grads).reshape(m // 8, 8, TILE), axis=0)

    early = x0.shape[1] // TILE

    @pl.loop(0, early)
    def _(j):
        span = pl.ds(pl.multiple_of(j * TILE, TILE), TILE)
        tile(j, x0[:, span], g0[:, span])

    @pl.loop(0, xa.shape[1] // TILE)
    def _(j):
        span = pl.ds(pl.multiple_of(j * TILE, TILE), TILE)
        x = jnp.concatenate([xa[:, span], xb[:, span]], axis=0)
        g = jnp.concatenate([ga[:, span], gb[:, span]], axis=0)
        tile(j + early, x, g)

    rows_b = hid_b.shape[0]
    last_ref[:rows_b, :] = hid_b[...]
    row = iota((16, last_ref.shape[1]), 0)
    coded = jnp.zeros(row.shape, F32)
    for i in range(3):
        rest = jnp.broadcast_to(jnp.sum(parts[i], keepdims=True), row.shape)
        for k in range(3):
            piece = rest.astype(BF16).astype(F32)
            coded = jnp.where(row == 3 * i + k, piece, coded)
            rest = rest - piece
    last_ref[rows_b:, :] = coded.astype(BF16)


def squares(rows_of_x, hid_a, hid_b):
    rows = hid_a.shape[0] + hid_b.shape[0]
    cols = hid_a.shape[1]
    width = rows_of_x[0].shape[1] + rows_of_x[2].shape[1]
    return pl.pallas_call(
        squares_kernel,
        in_specs=[VMEM] * 8,
        out_specs=(VMEM,) * 3,
        out_shape=in_vmem(
            ((hid_b.shape[0] + 16, cols), BF16), ((TILE, rows), BF16), ((TILE, rows), BF16)
        ),
        scratch_shapes=[pltpu.VMEM((cols, rows), BF16), pltpu.VMEM((3, 8, TILE), F32)],
        compiler_params=params(20),
        cost_estimate=pl.CostEstimate(
            flops=2 * rows * width * cols, bytes_accessed=4 * rows * width, transcendentals=0
        ),
        name="squares",
    )(*rows_of_x, hid_a, hid_b)


def final_kernel(entries, copies, sums, *refs):
    arrays, refs = refs[: -8], refs[-8:]
    xt_ref, gt_ref, out_ref, hid, coded, stage, in_sems, out_sems = refs
    for k, (i, row) in enumerate(sums):
        pltpu.make_async_copy(
            arrays[i].at[pl.ds(row, 16), pl.ds(0, 128)], coded.at[k], in_sems.at[8]
        ).start()

    def start(source):
        for owner, i, row, at, n in copies:
            if owner == source:
                pltpu.make_async_copy(
                    arrays[i].at[pl.ds(row, n), :],
                    hid.at[source, pl.ds(at, n), :],
                    in_sems.at[source],
                ).start()

    start(0)
    start(1)
    m = hid.shape[2] // 3
    pltpu.make_async_copy(coded, coded, in_sems.at[8]).wait()
    pieces = jnp.sum(coded[...].astype(F32), axis=0)
    factors = []
    for i in range(3):
        total = jnp.sum(pieces[3 * i : 3 * i + 3, :], axis=0, keepdims=True)
        factors.append(lax.rsqrt(total[:, 0:1] / entries + EPSILON))

    def store(slot, i):
        dz = jnp.where(i % 4 == 1, 3, jnp.where(i % 4 == 2, 1, jnp.where(i % 4 == 3, 2, 0)))
        at = pl.ds(pl.multiple_of(position(i // 4, dz) * m, m), m)
        return pltpu.make_async_copy(stage.at[slot], out_ref.at[:, :, at], out_sems.at[slot])

    @pl.loop(0, 8)
    def _(i):
        slot = i % 2
        pltpu.make_async_copy(hid.at[i], hid.at[i], in_sems.at[i]).wait()

        @pl.when(i == 0)
        def _():
            for source in range(2, 8):
                start(source)

        @pl.when(i >= 2)
        def _():
            store(slot, i - 2).wait()

        for k in range(3):
            lhs = gt_ref if k == 2 else xt_ref
            grads = jnp.dot(
                lhs[...], hid[i, :, k * m : (k + 1) * m], preferred_element_type=F32
            )
            stage[slot, k] = (grads * factors[k]).astype(BF16)
        store(slot, i).start()

    store(0, 6).wait()
    store(1, 7).wait()


def final(copies, sums, arrays, xt, gt, entries):
    rows = xt.shape[1]
    width = arrays[0].shape[1]
    m = width // 3
    return pl.pallas_call(
        functools.partial(final_kernel, entries, copies, sums),
        in_specs=[ANY] * len(arrays) + [VMEM] * 2,
        out_specs=HBM,
        out_shape=jax.ShapeDtypeStruct((3, TILE, 8 * m), BF16),
        scratch_shapes=[
            pltpu.VMEM((8, rows, width), BF16),
            pltpu.VMEM((8, 16, 128), BF16),
            pltpu.VMEM((2, 3, TILE, m), BF16),
            pltpu.SemaphoreType.DMA((9,)),
            pltpu.SemaphoreType.DMA((2,)),
        ],
        compiler_params=params(16),
        cost_estimate=pl.CostEstimate(
            flops=2 * rows * TILE * width * 8,
            bytes_accessed=4 * TILE * width * 8,
            transcendentals=0,
        ),
        name="final",
    )(*arrays, xt, gt)


def placed(source, array, row, group, offset, count, z, size):
    out = []
    while count:
        step = min(count, size - offset)
        out.append((source, array, row, ((group + z) % 4) * size + offset, step))
        row, count, group, offset = row + step, count - step, group + 1, 0
    merged = [out[0]]
    for item in out[1:]:
        s, a, r, at, c = merged[-1]
        if at + c == item[3]:
            merged[-1] = (s, a, r, at, c + item[4])
        else:
            merged.append(item)
    return merged


def cut(width, step):
    return tuple((at, min(step, width - at)) for at in range(0, width, step))


def body(tokens, out_grad, combine, expert_ids, expert_rank, gate_weight, up_weight, down_weight):
    width = tokens.shape[1]
    expert = ("y", "x")
    hot = lax.axis_size(expert)
    rows = hot * 2 * CAP
    n = rows // 2
    weights = (gate_weight[0], up_weight[0], down_weight[0])
    ids, comb = expert_ids.T, combine.T
    tiles = width // TILE
    sent = dispatch(ids, comb, expert_rank, tokens, out_grad, 0, EARLY, rows)
    ranks = after(expert_rank, sent)
    sent_rest = dispatch(ids, comb, ranks, tokens, out_grad, EARLY, tiles - EARLY, rows)
    early = EARLY * TILE

    near = near_z(sent)
    got = lax.all_to_all(
        sent_rest.reshape(hot, 2 * CAP, width - early), expert, split_axis=0, concat_axis=0, tiled=True
    )
    block = split_rows(got, (0,))
    far = far_z(near[1], near[2], n)
    block = after(block, far)
    four = [t.reshape(hot, 2 * CAP, early) for t in near + [jnp.concatenate(far)]]
    got = lax.all_to_all(
        jnp.concatenate(four, axis=1), expert, split_axis=0, concat_axis=0, tiled=True
    )
    whole = with_other([split_rows(got, (1, 0, 2, 3))])

    near = near_z(block)
    far = far_z(near[1], near[2], n)
    part, *x0 = acts(Rows(0, whole, "whole", (0, 1, 2, 3)), n, weights, False, 20)
    near = with_other(near)
    hid_a, xa, ga, *held = acts(
        Rows(early, near, "parts", (0, 1, 2)), n, weights, True, 20, part, 0, keep=True
    )
    far = with_other(after(tuple(far), hid_a))
    hid_b, xb, gb = acts(
        Rows(early, far, "parts", (3,)), n, held, True, 16, part, 6 * n, given=True
    )

    near_a = near_z(hid_a)
    hid_b, xt, gt = squares((*x0, xa, ga, xb, gb), hid_a, hid_b)
    half = hid_a.shape[0] // 2
    up_a, down_a = after((near_a[1], near_a[2]), hid_b)
    last = [
        hid_b,
        along(jnp.concatenate([up_a[:half], hid_b]), 1),
        along(jnp.concatenate([down_a[half:], hid_b]), 3),
        along(hid_b, 2),
    ]
    near_a = with_other(near_a)
    last = with_other(last)

    size = 2 * n
    copies, sums = [], []
    for a in range(2):
        for k, z in enumerate(NEAR_Z):
            copies += placed(4 * a + k, 3 * a + k, 0, 0, 0, 3 * size, z, size)
        mine, up, down, other = range(6 + 4 * a, 10 + 4 * a)
        copies += placed(4 * a, mine, 0, 3, 0, size, 0, size)
        copies += placed(4 * a + 1, up, half, 3, 0, size, 3, size)
        copies += placed(4 * a + 2, down, half, 3, 0, size, 1, size)
        copies += placed(4 * a + 3, up, 0, 0, 0, half, 2, size)
        copies += placed(4 * a + 3, down, 0, half // size, half % size, half, 2, size)
        copies += placed(4 * a + 3, other, 0, 3, 0, size, 2, size)
        sums += [(mine, size), (up, half + size), (down, half + size), (other, size)]
    entries = width * weights[0].shape[1] * 8
    return final(copies, sums, near_a + last, xt, gt, entries)[None]


def solution(mesh):
    fine = Mesh(mesh.devices.reshape(4, 4, 4, 2), ("y", "x", "z", "core"))
    expert, cuts = ("y", "x"), ("z", "core")
    tokens = P(expert + cuts, None)
    return jax.shard_map(
        body,
        mesh=fine,
        in_specs=(
            tokens,
            tokens,
            tokens,
            tokens,
            P(),
            P(expert, None, cuts),
            P(expert, None, cuts),
            P(expert, cuts, None),
        ),
        out_specs=P(expert, None, cuts, None),
        check_vma=False,
    )
```

```python
import functools

import jax
import jax.numpy as jnp
from jax import lax
from jax.experimental import pallas as pl
from jax.experimental.pallas import tpu as pltpu
from jax.sharding import Mesh
from jax.sharding import PartitionSpec as P

CAP = 4
ROW_BITS = 3
EPSILON = 1e-06
TILE = 896
AHEAD = 3
EARLY = 2
F32 = jnp.float32
BF16 = jnp.bfloat16
ANY = pl.BlockSpec(memory_space=pl.ANY)
HBM = pl.BlockSpec(memory_space=pltpu.HBM)
VMEM = pl.BlockSpec(memory_space=pltpu.VMEM)


def params(mib):
    return pltpu.CompilerParams(vmem_limit_bytes=mib * 1024 * 1024)


NEAR_Z = (0, 3, 1)


def in_hbm(*arrays):
    return [pltpu.with_memory_space_constraint(t, pltpu.HBM) for t in arrays]


def in_vmem(*shapes):
    return tuple(pltpu.VMEM(shape, dtype) for shape, dtype in shapes)


def iota(shape, dim):
    return lax.broadcasted_iota(jnp.int32, shape, dim)


def dispatch_kernel(first, tiles, *refs):
    small, (tok, grad, out_ref), refs = refs[:3], refs[3:6], refs[6:]
    ids_ref, comb_ref, rank_ref = refs[:3]
    both, sems = refs[3:]
    for k in range(3):
        pltpu.make_async_copy(small[k], refs[k], sems.at[tiles + k]).start()
    rows = out_ref.shape[0]
    toks = tok.shape[0]
    for j in range(tiles):
        span = pl.ds((first + j) * TILE, TILE)
        pltpu.make_async_copy(tok.at[:, span], both.at[j, pl.ds(0, toks), :], sems.at[j]).start()
        pltpu.make_async_copy(grad.at[:, span], both.at[j, pl.ds(toks, toks), :], sems.at[j]).start()
    for k in range(3):
        pltpu.make_async_copy(small[k], refs[k], sems.at[tiles + k]).wait()
    routed = rank_ref.shape[0]
    ranks = rank_ref[...].reshape(1, routed)
    expert_row = iota((rows, routed), 0) >> ROW_BITS
    ident = jnp.sum(
        jnp.where(ranks == expert_row, iota((rows, routed), 1), 0), axis=1, keepdims=True
    )
    hit = jnp.zeros((rows, toks), F32)
    comb = jnp.zeros((rows, toks), F32)
    for k in range(ids_ref.shape[0]):
        same = ids_ref[k : k + 1, :] == ident
        hit = jnp.where(same, 1.0, hit)
        comb = jnp.where(same, comb_ref[k : k + 1, :], comb)
    earlier = (iota((toks, toks), 0) < iota((toks, toks), 1)).astype(BF16)
    slot = jnp.dot(hit.astype(BF16), earlier, preferred_element_type=F32)
    row = iota((rows, toks), 0)
    want = (row & (CAP - 1)).astype(F32)
    is_grad = (row & CAP) != 0
    sel = jnp.where(slot == want, hit, 0.0)
    select = jnp.concatenate(
        [jnp.where(is_grad, 0.0, sel), jnp.where(is_grad, sel, 0.0)], axis=1
    ).astype(BF16)
    weight = jnp.sum(sel * comb, axis=1, keepdims=True)
    scale = jnp.where(is_grad[:, :1], weight, 1.0)
    for j in range(tiles):
        pltpu.make_async_copy(both.at[j], both.at[j], sems.at[j]).wait()
        picked = jnp.dot(select, both[j], preferred_element_type=F32)
        out_ref[:, j * TILE : (j + 1) * TILE] = (picked * scale).astype(BF16)


def dispatch(ids, comb, ranks, tokens, out_grad, first, tiles, rows):
    toks = tokens.shape[0]
    return pl.pallas_call(
        functools.partial(dispatch_kernel, first, tiles),
        in_specs=[HBM] * 5,
        out_specs=VMEM,
        out_shape=jax.ShapeDtypeStruct((rows, tiles * TILE), BF16),
        scratch_shapes=[
            pltpu.VMEM(ids.shape, ids.dtype),
            pltpu.VMEM(comb.shape, comb.dtype),
            pltpu.VMEM(ranks.shape, ranks.dtype),
            pltpu.VMEM((tiles, 2 * toks, TILE), BF16),
            pltpu.SemaphoreType.DMA((tiles + 3,)),
        ],
        compiler_params=params(20),
        cost_estimate=pl.CostEstimate(
            flops=tiles * 8 * toks * rows * TILE, bytes_accessed=tiles * 6 * toks * TILE, transcendentals=0
        ),
        name="dispatch",
    )(*in_hbm(ids, comb, ranks, tokens, out_grad))


def split_kernel(order, in_ref, out_ref):
    source_count, width = in_ref.shape[0], in_ref.shape[2]
    rows = source_count * 2 * CAP
    half = rows // 2
    r, c = iota((rows, rows), 0), iota((rows, rows), 1)
    group = r & (half - 1)
    source = (group & -CAP) * 2 + jnp.where(r >= half, CAP, 0) + (group & (CAP - 1))
    perm = (c == source).astype(BF16)
    for i, place in enumerate(order):
        block = in_ref[:, i * 2 * CAP : (i + 1) * 2 * CAP, :].reshape(rows, width)
        out_ref[place * rows : (place + 1) * rows, :] = jnp.dot(
            perm, block, preferred_element_type=F32
        ).astype(BF16)


def split_rows(block, order):
    rows = block.shape[0] * block.shape[1]
    return pl.pallas_call(
        functools.partial(split_kernel, order),
        in_specs=[VMEM],
        out_specs=VMEM,
        out_shape=jax.ShapeDtypeStruct((rows, block.shape[2]), BF16),
        compiler_params=params(16),
        name="split_rows",
    )(block)


def shift(n, k):
    return [(i, (i + k) % n) for i in range(n)]


def along(x, k):
    return lax.ppermute(x, "z", shift(4, k))


def swap(x):
    return lax.ppermute(x, "core", shift(2, 1))


def after(x, dep):
    return lax.optimization_barrier((x, dep))[0]


def near_z(block):
    return [block, along(block, 1), along(block, 3)]


def far_z(up, down, half):
    return [along(up[:half], 1), along(down[half:], 3)]


def with_other(mine):
    return list(mine) + [swap(t) for t in mine]


def position(dc, dz):
    z = lax.rem(lax.axis_index("z") + dz, 4)
    return z * 2 + lax.rem(lax.axis_index("core") + dc, 2)


class Rows:
    def __init__(self, first, arrays, kind, groups):
        self.first, self.arrays, self.kind, self.groups = first, arrays, kind, groups
        self.width = arrays[0].shape[1]

    def pinned(self):
        count = len(self.arrays) // 2 if self.kind == "parts" and self.groups[0] == 0 else 0
        return in_hbm(*self.arrays[:count]) + list(self.arrays[count:])

    def sources(self, refs, a, n):
        refs = refs[a * len(refs) // 2 : (a + 1) * len(refs) // 2]
        out = []
        for group in self.groups:
            if self.kind == "whole":
                out.append((group, refs[0], 2 * n * group, refs[0], 2 * n * group + n))
            elif group < 3:
                ref = refs[(1, 0, 2)[group]]
                out.append((group, ref, 0, ref, n))
            else:
                out.append((group, refs[-2], 0, refs[-1], 0))
        return out

    def start(self, refs, x_s, g_s, column, width, x_sem, g_sem):
        span = pl.ds(column, width)
        n = x_s.shape[0] // (2 * len(self.groups))
        core = lax.axis_index("core")
        for a in range(2):
            here = core if a == 0 else 1 - core
            for group, x, x_row, g, g_row in self.sources(refs, a, n):
                at = pl.multiple_of((group - self.groups[0]) * 2 * n + here * n, n)
                at = pl.ds(at, n)
                pltpu.make_async_copy(x.at[pl.ds(x_row, n), span], x_s.at[at, :], x_sem).start()
                pltpu.make_async_copy(g.at[pl.ds(g_row, n), span], g_s.at[at, :], g_sem).start()


def acts_kernel(rows_of, skip, last, keep, given, *refs):
    blocks, refs = refs[: len(rows_of.arrays)], refs[len(rows_of.arrays) :]
    weights, refs = refs[:3], refs[3:]
    if skip is not None:
        before, refs = refs[0], refs[1:]
    out_ref, x_s, g_s = refs[:3]
    refs = refs[3:]
    if given:
        held = weights
    else:
        held, refs = refs[:3], refs[3:]
    sems, acc_sem = refs[:2]
    acc = refs[2] if last else out_ref
    rows = acc.shape[1]
    count = rows_of.width // TILE
    if skip is not None:
        pltpu.make_async_copy(before.at[:, pl.ds(skip, rows), :], acc, acc_sem).start()

    def views(j):
        span = pl.ds(j * TILE, TILE)
        return (
            x_s.at[:, span], g_s.at[:, span], held[0].at[span, :], held[1].at[span, :], held[2].at[:, span]
        )

    def start(j):
        x, g, wg, wu, wd = views(j)
        span = pl.ds(rows_of.first + j * TILE, TILE)
        if not given:
            pltpu.make_async_copy(weights[0].at[span, :], wg, sems.at[2, j]).start()
            pltpu.make_async_copy(weights[1].at[span, :], wu, sems.at[3, j]).start()
        rows_of.start(blocks, x, g, j * TILE, TILE, sems.at[0, j], sems.at[1, j])
        if not given:
            pltpu.make_async_copy(weights[2].at[:, span], wd, sems.at[4, j]).start()

    for j in range(min(AHEAD, count)):
        start(j)
    if skip is not None:
        pltpu.make_async_copy(acc, acc, acc_sem).wait()
    for j in range(count):
        x, g, wg, wu, wd = views(j)
        for k, ref in enumerate((x, g) if given else (x, g, wg, wu, wd)):
            pltpu.make_async_copy(ref, ref, sems.at[k, j]).wait()
        if j + AHEAD < count:
            start(j + AHEAD)
        new = (
            jnp.dot(x[...], wg[...], preferred_element_type=F32),
            jnp.dot(x[...], wu[...], preferred_element_type=F32),
            lax.dot_general(
                g[...], wd[...], (((1,), (1,)), ((), ())), preferred_element_type=F32
            ),
        )
        for k in range(3):
            if j == 0 and skip is None:
                acc[k] = new[k]
            else:
                acc[k] += new[k]

    if last:
        m = acc.shape[2]
        step = 64

        @pl.loop(0, rows // step)
        def _(i):
            at = pl.ds(pl.multiple_of(i * step, step), step)
            gate, up, act = acc[0, at, :], acc[1, at, :], acc[2, at, :]
            sig = jax.nn.sigmoid(gate)
            out_ref[at, 0:m] = (act * up * sig * (1.0 + gate * (1.0 - sig))).astype(BF16)
            out_ref[at, m : 2 * m] = (act * gate * sig).astype(BF16)
            out_ref[at, 2 * m : 3 * m] = (gate * sig * up).astype(BF16)


def acts(rows_of, n, weights, last, mib, before=None, skip=None, keep=False, given=False):
    m = weights[2].shape[0]
    rows = 2 * n * len(rows_of.groups)
    width = rows_of.width
    out = ((rows, 3 * m), BF16) if last else ((3, rows, m), F32)
    outs = [out, ((rows, width), BF16), ((rows, width), BF16)]
    held = [((width, m), BF16), ((width, m), BF16), ((m, width), BF16)]
    scratch = []
    if keep:
        outs += held
    elif not given:
        scratch += [pltpu.VMEM(*shape) for shape in held]
    scratch += [pltpu.SemaphoreType.DMA((5, width // TILE)), pltpu.SemaphoreType.DMA(())]
    if last:
        scratch.append(pltpu.VMEM((3, rows, m), F32))
    extra = [] if before is None else [before]
    return pl.pallas_call(
        functools.partial(acts_kernel, rows_of, skip, last, keep, given),
        in_specs=[ANY] * len(rows_of.arrays) + [VMEM if given else HBM] * 3 + [VMEM] * len(extra),
        out_specs=(VMEM,) * len(outs),
        out_shape=in_vmem(*outs),
        scratch_shapes=scratch,
        compiler_params=params(mib),
        cost_estimate=pl.CostEstimate(
            flops=6 * rows * width * m,
            bytes_accessed=4 * rows * width + 6 * m * width,
            transcendentals=0,
        ),
        name="acts",
    )(*rows_of.pinned(), *(weights if given else in_hbm(*weights)), *extra)


def squares_kernel(x0, g0, xa, ga, xb, gb, hid_a, hid_b, last_ref, xt_ref, gt_ref, hid_t, parts):
    m = hid_a.shape[1] // 3
    rows_a = hid_a.shape[0]
    hid_t[:, :rows_a] = hid_a[...].T
    hid_t[:, rows_a:] = hid_b[...].T
    parts[...] = jnp.zeros_like(parts)
    mine = position(0, 0)

    def tile(j, x, g):
        @pl.when(j == mine)
        def _():
            xt_ref[...] = x.T
            gt_ref[...] = g.T

        both = jnp.dot(hid_t[: 2 * m, :], x, preferred_element_type=F32)
        down = jnp.dot(hid_t[2 * m :, :], g, preferred_element_type=F32)
        for i, grads in enumerate((both[:m], both[m:], down)):
            parts[i] += jnp.sum((grads * grads).reshape(m // 8, 8, TILE), axis=0)

    early = x0.shape[1] // TILE

    @pl.loop(0, early)
    def _(j):
        span = pl.ds(pl.multiple_of(j * TILE, TILE), TILE)
        tile(j, x0[:, span], g0[:, span])

    @pl.loop(0, xa.shape[1] // TILE)
    def _(j):
        span = pl.ds(pl.multiple_of(j * TILE, TILE), TILE)
        x = jnp.concatenate([xa[:, span], xb[:, span]], axis=0)
        g = jnp.concatenate([ga[:, span], gb[:, span]], axis=0)
        tile(j + early, x, g)

    rows_b = hid_b.shape[0]
    last_ref[:rows_b, :] = hid_b[...]
    row = iota((16, last_ref.shape[1]), 0)
    coded = jnp.zeros(row.shape, F32)
    for i in range(3):
        rest = jnp.broadcast_to(jnp.sum(parts[i], keepdims=True), row.shape)
        for k in range(3):
            piece = rest.astype(BF16).astype(F32)
            coded = jnp.where(row == 3 * i + k, piece, coded)
            rest = rest - piece
    last_ref[rows_b:, :] = coded.astype(BF16)


def squares(rows_of_x, hid_a, hid_b):
    rows = hid_a.shape[0] + hid_b.shape[0]
    cols = hid_a.shape[1]
    width = rows_of_x[0].shape[1] + rows_of_x[2].shape[1]
    return pl.pallas_call(
        squares_kernel,
        in_specs=[VMEM] * 8,
        out_specs=(VMEM,) * 3,
        out_shape=in_vmem(
            ((hid_b.shape[0] + 16, cols), BF16), ((TILE, rows), BF16), ((TILE, rows), BF16)
        ),
        scratch_shapes=[pltpu.VMEM((cols, rows), BF16), pltpu.VMEM((3, 8, TILE), F32)],
        compiler_params=params(20),
        cost_estimate=pl.CostEstimate(
            flops=2 * rows * width * cols, bytes_accessed=4 * rows * width, transcendentals=0
        ),
        name="squares",
    )(*rows_of_x, hid_a, hid_b)


def start_copies(copies, source, slot, arrays, hid, sems):
    for owner, i, row, at, n in copies:
        if owner == source:
            pltpu.make_async_copy(
                arrays[i].at[pl.ds(row, n), :], hid.at[slot, pl.ds(at, n), :], sems.at[slot]
            ).start()


def wait_rows(hid, slot, rows, sems):
    ref = hid.at[slot, pl.ds(0, rows), :]
    pltpu.make_async_copy(ref, ref, sems.at[slot]).wait()


def early_kernel(copies, missing, *refs):
    arrays, (xt_ref, gt_ref, pre_ref, hid, sems) = refs[:-5], refs[-5:]
    count, rows = hid.shape[0], hid.shape[1]
    m = hid.shape[2] // 3
    for k in range(count):
        start_copies(copies, k, k, arrays, hid, sems)
        if missing[k] is not None:
            at, n = missing[k]
            hid[k, at : at + n, :] = jnp.zeros((n, 3 * m), BF16)
    for k in range(count):
        wait_rows(hid, k, rows - (0 if missing[k] is None else missing[k][1]), sems)
        for i in range(3):
            lhs = gt_ref if i == 2 else xt_ref
            pre_ref[k, i] = jnp.dot(
                lhs[...], hid[k, :, i * m : (i + 1) * m], preferred_element_type=F32
            )


def early_products(copies, missing, arrays, xt, gt):
    rows = xt.shape[1]
    width = arrays[0].shape[1]
    count = len(missing)
    return pl.pallas_call(
        functools.partial(early_kernel, copies, missing),
        in_specs=[ANY] * len(arrays) + [VMEM] * 2,
        out_specs=VMEM,
        out_shape=in_vmem(((count, 3, TILE, width // 3), F32))[0],
        scratch_shapes=[
            pltpu.VMEM((count, rows, width), BF16),
            pltpu.SemaphoreType.DMA((count,)),
        ],
        compiler_params=params(12),
        cost_estimate=pl.CostEstimate(
            flops=2 * rows * TILE * width * count,
            bytes_accessed=2 * rows * width * count,
            transcendentals=0,
        ),
        name="early_products",
    )(*arrays, xt, gt)


def final_kernel(entries, plan, copies, sums, *refs):
    arrays, refs = refs[:-9], refs[-9:]
    pre_ref, xt_ref, gt_ref, out_ref, hid, coded, stage, in_sems, out_sems = refs
    for k, (i, row) in enumerate(sums):
        pltpu.make_async_copy(
            arrays[i].at[pl.ds(row, 16), pl.ds(0, 128)], coded.at[k], in_sems.at[8]
        ).start()
    for source, _, _, rows in plan:
        if rows is not None:
            start_copies(copies, source, source, arrays, hid, in_sems)
    m = hid.shape[2] // 3
    pltpu.make_async_copy(coded, coded, in_sems.at[8]).wait()
    pieces = jnp.sum(coded[...].astype(F32), axis=0)
    factors = []
    for i in range(3):
        total = jnp.sum(pieces[3 * i : 3 * i + 3, :], axis=0, keepdims=True)
        factors.append(lax.rsqrt(total[:, 0:1] / entries + EPSILON))

    def store(slot, source):
        at = position(source // 4, (0, 3, 1, 2)[source % 4])
        at = pl.ds(pl.multiple_of(at * m, m), m)
        return pltpu.make_async_copy(stage.at[slot], out_ref.at[:, :, at], out_sems.at[slot])

    slots = stage.shape[0]
    for step, (source, early, at, rows) in enumerate(plan):
        slot = step % slots
        if step >= slots:
            store(slot, plan[step - slots][0]).wait()
        if rows is not None:
            wait_rows(hid, source, rows, in_sems)
        for i in range(3):
            lhs = gt_ref if i == 2 else xt_ref
            grads = None if early is None else pre_ref[early, i]
            if rows is not None:
                more = jnp.dot(
                    lhs[:, at : at + rows],
                    hid[source, :rows, i * m : (i + 1) * m],
                    preferred_element_type=F32,
                )
                grads = more if grads is None else grads + more
            stage[slot, i] = (grads * factors[i]).astype(BF16)
        store(slot, source).start()
    for step in range(len(plan) - slots, len(plan)):
        store(step % slots, plan[step][0]).wait()


def final(plan, copies, sums, arrays, pre, xt, gt, entries):
    rows = xt.shape[1]
    width = arrays[0].shape[1]
    m = width // 3
    return pl.pallas_call(
        functools.partial(final_kernel, entries, plan, copies, sums),
        in_specs=[ANY] * len(arrays) + [VMEM] * 3,
        out_specs=HBM,
        out_shape=jax.ShapeDtypeStruct((3, TILE, 8 * m), BF16),
        scratch_shapes=[
            pltpu.VMEM((8, rows, width), BF16),
            pltpu.VMEM((8, 16, 128), BF16),
            pltpu.VMEM((3, 3, TILE, m), BF16),
            pltpu.SemaphoreType.DMA((9,)),
            pltpu.SemaphoreType.DMA((3,)),
        ],
        compiler_params=params(20),
        cost_estimate=pl.CostEstimate(
            flops=rows * TILE * width * 8,
            bytes_accessed=4 * TILE * width * 8,
            transcendentals=0,
        ),
        name="final",
    )(*arrays, pre, xt, gt)


def placed(source, array, row, group, offset, count, z, size):
    out = []
    while count:
        step = min(count, size - offset)
        out.append((source, array, row, ((group + z) % 4) * size + offset, step))
        row, count, group, offset = row + step, count - step, group + 1, 0
    merged = [out[0]]
    for item in out[1:]:
        s, a, r, at, c = merged[-1]
        if at + c == item[3]:
            merged[-1] = (s, a, r, at, c + item[4])
        else:
            merged.append(item)
    return merged


def cut(width, step):
    return tuple((at, min(step, width - at)) for at in range(0, width, step))


def body(tokens, out_grad, combine, expert_ids, expert_rank, gate_weight, up_weight, down_weight):
    width = tokens.shape[1]
    expert = ("y", "x")
    hot = lax.axis_size(expert)
    rows = hot * 2 * CAP
    n = rows // 2
    weights = (gate_weight[0], up_weight[0], down_weight[0])
    ids, comb = expert_ids.T, combine.T
    tiles = width // TILE
    sent_rest = dispatch(ids, comb, expert_rank, tokens, out_grad, EARLY, tiles - EARLY, rows)
    ranks = after(expert_rank, sent_rest)
    sent = dispatch(ids, comb, ranks, tokens, out_grad, 0, EARLY, rows)
    early = EARLY * TILE

    near = near_z(sent)
    got = lax.all_to_all(
        sent_rest.reshape(hot, 2 * CAP, width - early), expert, split_axis=0, concat_axis=0, tiled=True
    )
    block = split_rows(got, (0,))
    far = far_z(near[1], near[2], n)
    block = after(block, far)
    near = list(after(tuple(near), block))
    four = [t.reshape(hot, 2 * CAP, early) for t in near + [jnp.concatenate(far)]]
    got = lax.all_to_all(
        jnp.concatenate(four, axis=1), expert, split_axis=0, concat_axis=0, tiled=True
    )
    whole = with_other([split_rows(got, (1, 0, 2, 3))])

    near = near_z(block)
    far = far_z(near[1], near[2], n)
    part, *x0 = acts(Rows(0, whole, "whole", (0, 1, 2, 3)), n, weights, False, 20)
    near = with_other(near)
    hid_a, xa, ga, *held = acts(
        Rows(early, near, "parts", (0, 1, 2)), n, weights, True, 20, part, 0, keep=True
    )
    far = with_other(after(tuple(far), hid_a))
    hid_b, xb, gb = acts(
        Rows(early, far, "parts", (3,)), n, held, True, 16, part, 6 * n, given=True
    )

    near_a = near_z(hid_a)
    hid_b, xt, gt = squares((*x0, xa, ga, xb, gb), hid_a, hid_b)
    half = hid_a.shape[0] // 2
    up_a, down_a = after((near_a[1], near_a[2]), hid_b)
    last = [
        hid_b,
        along(jnp.concatenate([up_a[:half], hid_b]), 1),
        along(jnp.concatenate([down_a[half:], hid_b]), 3),
        along(hid_b, 2),
    ]
    near_a = with_other([hid_a, up_a, down_a])

    size = 2 * n
    other = swap(hid_b)
    copies, missing = [], []
    for a in range(2):
        for k, z in enumerate(NEAR_Z):
            copies += placed(3 * a + k, 3 * a + k, 0, 0, 0, 3 * size, z, size)
            missing.append(None if z == 0 else ((3 + z) % 4 * size, size))
        copies += placed(3 * a, 6 + a, 0, 3, 0, size, 0, size)
    pre = early_products(copies, missing, near_a + [hid_b, other], xt, gt)

    last = last[1:]
    last = [hid_b, other] + last + [swap(t) for t in after(last, pre)]
    copies, sums, plan = [], [(0, size), (1, size)], []
    for a in range(2):
        up, down, far = range(2 + 3 * a, 5 + 3 * a)
        plan.append((4 * a, 3 * a, 0, None))
        plan.append((4 * a + 1, 3 * a + 1, 2 * size, size))
        plan.append((4 * a + 2, 3 * a + 2, 0, size))
        plan.append((4 * a + 3, None, 0, 4 * size))
        copies += [(4 * a + 1, up, half, 0, size), (4 * a + 2, down, half, 0, size)]
        copies += placed(4 * a + 3, up, 0, 0, 0, half, 2, size)
        copies += placed(4 * a + 3, down, 0, half // size, half % size, half, 2, size)
        copies += placed(4 * a + 3, far, 0, 3, 0, size, 2, size)
        sums += [(up, half + size), (down, half + size), (far, size)]
    plan.sort(key=lambda step: step[0] % 4)
    entries = width * weights[0].shape[1] * 8
    return final(plan, copies, sums, last, pre, xt, gt, entries)[None]


def solution(mesh):
    fine = Mesh(mesh.devices.reshape(4, 4, 4, 2), ("y", "x", "z", "core"))
    expert, cuts = ("y", "x"), ("z", "core")
    tokens = P(expert + cuts, None)
    return jax.shard_map(
        body,
        mesh=fine,
        in_specs=(
            tokens,
            tokens,
            tokens,
            tokens,
            P(),
            P(expert, None, cuts),
            P(expert, None, cuts),
            P(expert, cuts, None),
        ),
        out_specs=P(expert, None, cuts, None),
        check_vma=False,
    )
```

```python
import functools

import jax
import jax.numpy as jnp
from jax import lax
from jax.experimental import pallas as pl
from jax.experimental.pallas import tpu as pltpu
from jax.sharding import Mesh
from jax.sharding import PartitionSpec as P

CAP = 4
ROW_BITS = 3
EPSILON = 1e-06
TILE = 896
AHEAD = 3
EARLY = 2
F32 = jnp.float32
BF16 = jnp.bfloat16
ANY = pl.BlockSpec(memory_space=pl.ANY)
HBM = pl.BlockSpec(memory_space=pltpu.HBM)
VMEM = pl.BlockSpec(memory_space=pltpu.VMEM)


def params(mib):
    return pltpu.CompilerParams(vmem_limit_bytes=mib * 1024 * 1024)


NEAR_Z = (0, 3, 1)


def in_hbm(*arrays):
    return [pltpu.with_memory_space_constraint(t, pltpu.HBM) for t in arrays]


def in_vmem(*shapes):
    return tuple(pltpu.VMEM(shape, dtype) for shape, dtype in shapes)


def iota(shape, dim):
    return lax.broadcasted_iota(jnp.int32, shape, dim)


def dispatch_kernel(first, tiles, *refs):
    small, (tok, grad, out_ref), refs = refs[:3], refs[3:6], refs[6:]
    ids_ref, comb_ref, rank_ref = refs[:3]
    both, sems = refs[3:]
    for k in range(3):
        pltpu.make_async_copy(small[k], refs[k], sems.at[tiles + k]).start()
    rows = out_ref.shape[0]
    toks = tok.shape[0]
    for j in range(tiles):
        span = pl.ds((first + j) * TILE, TILE)
        pltpu.make_async_copy(tok.at[:, span], both.at[j, pl.ds(0, toks), :], sems.at[j]).start()
        pltpu.make_async_copy(grad.at[:, span], both.at[j, pl.ds(toks, toks), :], sems.at[j]).start()
    for k in range(3):
        pltpu.make_async_copy(small[k], refs[k], sems.at[tiles + k]).wait()
    routed = rank_ref.shape[0]
    ranks = rank_ref[...].reshape(1, routed)
    expert_row = iota((rows, routed), 0) >> ROW_BITS
    ident = jnp.sum(
        jnp.where(ranks == expert_row, iota((rows, routed), 1), 0), axis=1, keepdims=True
    )
    hit = jnp.zeros((rows, toks), F32)
    comb = jnp.zeros((rows, toks), F32)
    for k in range(ids_ref.shape[0]):
        same = ids_ref[k : k + 1, :] == ident
        hit = jnp.where(same, 1.0, hit)
        comb = jnp.where(same, comb_ref[k : k + 1, :], comb)
    earlier = (iota((toks, toks), 0) < iota((toks, toks), 1)).astype(BF16)
    slot = jnp.dot(hit.astype(BF16), earlier, preferred_element_type=F32)
    row = iota((rows, toks), 0)
    want = (row & (CAP - 1)).astype(F32)
    is_grad = (row & CAP) != 0
    sel = jnp.where(slot == want, hit, 0.0)
    select = jnp.concatenate(
        [jnp.where(is_grad, 0.0, sel), jnp.where(is_grad, sel, 0.0)], axis=1
    ).astype(BF16)
    weight = jnp.sum(sel * comb, axis=1, keepdims=True)
    scale = jnp.where(is_grad[:, :1], weight, 1.0)
    for j in range(tiles):
        pltpu.make_async_copy(both.at[j], both.at[j], sems.at[j]).wait()
        picked = jnp.dot(select, both[j], preferred_element_type=F32)
        out_ref[:, j * TILE : (j + 1) * TILE] = (picked * scale).astype(BF16)


def dispatch(ids, comb, ranks, tokens, out_grad, first, tiles, rows):
    toks = tokens.shape[0]
    return pl.pallas_call(
        functools.partial(dispatch_kernel, first, tiles),
        in_specs=[HBM] * 5,
        out_specs=VMEM,
        out_shape=jax.ShapeDtypeStruct((rows, tiles * TILE), BF16),
        scratch_shapes=[
            pltpu.VMEM(ids.shape, ids.dtype),
            pltpu.VMEM(comb.shape, comb.dtype),
            pltpu.VMEM(ranks.shape, ranks.dtype),
            pltpu.VMEM((tiles, 2 * toks, TILE), BF16),
            pltpu.SemaphoreType.DMA((tiles + 3,)),
        ],
        compiler_params=params(20),
        cost_estimate=pl.CostEstimate(
            flops=tiles * 8 * toks * rows * TILE, bytes_accessed=tiles * 6 * toks * TILE, transcendentals=0
        ),
        name="dispatch",
    )(*in_hbm(ids, comb, ranks, tokens, out_grad))


def split_kernel(order, in_ref, out_ref):
    source_count, width = in_ref.shape[0], in_ref.shape[2]
    rows = source_count * 2 * CAP
    half = rows // 2
    r, c = iota((rows, rows), 0), iota((rows, rows), 1)
    group = r & (half - 1)
    source = (group & -CAP) * 2 + jnp.where(r >= half, CAP, 0) + (group & (CAP - 1))
    perm = (c == source).astype(BF16)
    for i, place in enumerate(order):
        block = in_ref[:, i * 2 * CAP : (i + 1) * 2 * CAP, :].reshape(rows, width)
        out_ref[place * rows : (place + 1) * rows, :] = jnp.dot(
            perm, block, preferred_element_type=F32
        ).astype(BF16)


def split_rows(block, order):
    rows = block.shape[0] * block.shape[1]
    return pl.pallas_call(
        functools.partial(split_kernel, order),
        in_specs=[VMEM],
        out_specs=VMEM,
        out_shape=jax.ShapeDtypeStruct((rows, block.shape[2]), BF16),
        compiler_params=params(16),
        name="split_rows",
    )(block)


def pack_kernel(*refs):
    blocks, first, second, out = refs[:-3], refs[-3], refs[-2], refs[-1]
    hot, _, width = out.shape
    per = 2 * CAP
    for i, ref in enumerate(blocks):
        out[:, i * per : (i + 1) * per, :] = ref[...].reshape(hot, per, width)
    at = len(blocks) * per
    out[: hot // 2, at:, :] = first[...].reshape(hot // 2, per, width)
    out[hot // 2 :, at:, :] = second[...].reshape(hot // 2, per, width)


def pack(blocks, first, second, hot):
    per, width = 2 * CAP, first.shape[1]
    return pl.pallas_call(
        pack_kernel,
        in_specs=[VMEM] * (len(blocks) + 2),
        out_specs=VMEM,
        out_shape=jax.ShapeDtypeStruct((hot, (len(blocks) + 1) * per, width), BF16),
        compiler_params=params(16),
        name="pack",
    )(*blocks, first, second)


def shift(n, k):
    return [(i, (i + k) % n) for i in range(n)]


def along(x, k):
    return lax.ppermute(x, "z", shift(4, k))


def swap(x):
    return lax.ppermute(x, "core", shift(2, 1))


def after(x, dep):
    return lax.optimization_barrier((x, dep))[0]


def near_z(block):
    return [block, along(block, 1), along(block, 3)]


def far_z(up, down, half):
    return [along(up[:half], 1), along(down[half:], 3)]


def with_other(mine):
    return list(mine) + [swap(t) for t in mine]


def position(dc, dz):
    z = lax.rem(lax.axis_index("z") + dz, 4)
    return z * 2 + lax.rem(lax.axis_index("core") + dc, 2)


class Rows:
    def __init__(self, first, arrays, kind, groups):
        self.first, self.arrays, self.kind, self.groups = first, arrays, kind, groups
        self.width = arrays[0].shape[1]

    def pinned(self):
        count = len(self.arrays) // 2 if self.kind == "parts" and self.groups[0] == 0 else 0
        return in_hbm(*self.arrays[:count]) + list(self.arrays[count:])

    def sources(self, refs, a, n):
        refs = refs[a * len(refs) // 2 : (a + 1) * len(refs) // 2]
        out = []
        for group in self.groups:
            if self.kind == "whole":
                out.append((group, refs[0], 2 * n * group, refs[0], 2 * n * group + n))
            elif group < 3:
                ref = refs[(1, 0, 2)[group]]
                out.append((group, ref, 0, ref, n))
            else:
                out.append((group, refs[-2], 0, refs[-1], 0))
        return out

    def start(self, refs, x_s, g_s, column, width, x_sem, g_sem):
        span = pl.ds(column, width)
        n = x_s.shape[0] // (2 * len(self.groups))
        core = lax.axis_index("core")
        for a in range(2):
            here = core if a == 0 else 1 - core
            for group, x, x_row, g, g_row in self.sources(refs, a, n):
                at = pl.multiple_of((group - self.groups[0]) * 2 * n + here * n, n)
                at = pl.ds(at, n)
                pltpu.make_async_copy(x.at[pl.ds(x_row, n), span], x_s.at[at, :], x_sem).start()
                pltpu.make_async_copy(g.at[pl.ds(g_row, n), span], g_s.at[at, :], g_sem).start()


def acts_kernel(rows_of, skip, last, keep, given, *refs):
    blocks, refs = refs[: len(rows_of.arrays)], refs[len(rows_of.arrays) :]
    weights, refs = refs[:3], refs[3:]
    if skip is not None:
        before, refs = refs[0], refs[1:]
    out_ref, x_s, g_s = refs[:3]
    refs = refs[3:]
    if given:
        held = weights
    else:
        held, refs = refs[:3], refs[3:]
    sems, acc_sem = refs[:2]
    acc = refs[2] if last else out_ref
    rows = acc.shape[1]
    count = rows_of.width // TILE
    if skip is not None:
        pltpu.make_async_copy(before.at[:, pl.ds(skip, rows), :], acc, acc_sem).start()

    def views(j):
        span = pl.ds(j * TILE, TILE)
        return (
            x_s.at[:, span], g_s.at[:, span], held[0].at[span, :], held[1].at[span, :], held[2].at[:, span]
        )

    def start(j):
        x, g, wg, wu, wd = views(j)
        span = pl.ds(rows_of.first + j * TILE, TILE)
        if not given:
            pltpu.make_async_copy(weights[0].at[span, :], wg, sems.at[2, j]).start()
            pltpu.make_async_copy(weights[1].at[span, :], wu, sems.at[3, j]).start()
        rows_of.start(blocks, x, g, j * TILE, TILE, sems.at[0, j], sems.at[1, j])
        if not given:
            pltpu.make_async_copy(weights[2].at[:, span], wd, sems.at[4, j]).start()

    for j in range(min(AHEAD, count)):
        start(j)
    if skip is not None:
        pltpu.make_async_copy(acc, acc, acc_sem).wait()
    for j in range(count):
        x, g, wg, wu, wd = views(j)
        for k, ref in enumerate((x, g) if given else (x, g, wg, wu, wd)):
            pltpu.make_async_copy(ref, ref, sems.at[k, j]).wait()
        if j + AHEAD < count:
            start(j + AHEAD)
        new = (
            jnp.dot(x[...], wg[...], preferred_element_type=F32),
            jnp.dot(x[...], wu[...], preferred_element_type=F32),
            lax.dot_general(
                g[...], wd[...], (((1,), (1,)), ((), ())), preferred_element_type=F32
            ),
        )
        for k in range(3):
            if j == 0 and skip is None:
                acc[k] = new[k]
            else:
                acc[k] += new[k]

    if last:
        m = acc.shape[2]
        step = 64

        @pl.loop(0, rows // step)
        def _(i):
            at = pl.ds(pl.multiple_of(i * step, step), step)
            gate, up, act = acc[0, at, :], acc[1, at, :], acc[2, at, :]
            sig = jax.nn.sigmoid(gate)
            out_ref[at, 0:m] = (act * up * sig * (1.0 + gate * (1.0 - sig))).astype(BF16)
            out_ref[at, m : 2 * m] = (act * gate * sig).astype(BF16)
            out_ref[at, 2 * m : 3 * m] = (gate * sig * up).astype(BF16)


def acts(rows_of, n, weights, last, mib, before=None, skip=None, keep=False, given=False):
    m = weights[2].shape[0]
    rows = 2 * n * len(rows_of.groups)
    width = rows_of.width
    out = ((rows, 3 * m), BF16) if last else ((3, rows, m), F32)
    outs = [out, ((rows, width), BF16), ((rows, width), BF16)]
    held = [((width, m), BF16), ((width, m), BF16), ((m, width), BF16)]
    scratch = []
    if keep:
        outs += held
    elif not given:
        scratch += [pltpu.VMEM(*shape) for shape in held]
    scratch += [pltpu.SemaphoreType.DMA((5, width // TILE)), pltpu.SemaphoreType.DMA(())]
    if last:
        scratch.append(pltpu.VMEM((3, rows, m), F32))
    extra = [] if before is None else [before]
    return pl.pallas_call(
        functools.partial(acts_kernel, rows_of, skip, last, keep, given),
        in_specs=[ANY] * len(rows_of.arrays) + [VMEM if given else HBM] * 3 + [VMEM] * len(extra),
        out_specs=(VMEM,) * len(outs),
        out_shape=in_vmem(*outs),
        scratch_shapes=scratch,
        compiler_params=params(mib),
        cost_estimate=pl.CostEstimate(
            flops=6 * rows * width * m,
            bytes_accessed=4 * rows * width + 6 * m * width,
            transcendentals=0,
        ),
        name="acts",
    )(*rows_of.pinned(), *(weights if given else in_hbm(*weights)), *extra)


def squares_kernel(x0, g0, xa, ga, xb, gb, hid_a, hid_b, last_ref, xt_ref, gt_ref, hid_t, parts):
    m = hid_a.shape[1] // 3
    rows_a = hid_a.shape[0]
    hid_t[:, :rows_a] = hid_a[...].T
    hid_t[:, rows_a:] = hid_b[...].T
    parts[...] = jnp.zeros_like(parts)
    mine = position(0, 0)

    def tile(j, x, g):
        @pl.when(j == mine)
        def _():
            xt_ref[...] = x.T
            gt_ref[...] = g.T

        both = jnp.dot(hid_t[: 2 * m, :], x, preferred_element_type=F32)
        down = jnp.dot(hid_t[2 * m :, :], g, preferred_element_type=F32)
        for i, grads in enumerate((both[:m], both[m:], down)):
            parts[i] += jnp.sum((grads * grads).reshape(m // 8, 8, TILE), axis=0)

    early = x0.shape[1] // TILE

    @pl.loop(0, early)
    def _(j):
        span = pl.ds(pl.multiple_of(j * TILE, TILE), TILE)
        tile(j, x0[:, span], g0[:, span])

    @pl.loop(0, xa.shape[1] // TILE)
    def _(j):
        span = pl.ds(pl.multiple_of(j * TILE, TILE), TILE)
        x = jnp.concatenate([xa[:, span], xb[:, span]], axis=0)
        g = jnp.concatenate([ga[:, span], gb[:, span]], axis=0)
        tile(j + early, x, g)

    rows_b = hid_b.shape[0]
    last_ref[:rows_b, :] = hid_b[...]
    row = iota((16, last_ref.shape[1]), 0)
    coded = jnp.zeros(row.shape, F32)
    for i in range(3):
        rest = jnp.broadcast_to(jnp.sum(parts[i], keepdims=True), row.shape)
        for k in range(3):
            piece = rest.astype(BF16).astype(F32)
            coded = jnp.where(row == 3 * i + k, piece, coded)
            rest = rest - piece
    last_ref[rows_b:, :] = coded.astype(BF16)


def squares(rows_of_x, hid_a, hid_b):
    rows = hid_a.shape[0] + hid_b.shape[0]
    cols = hid_a.shape[1]
    width = rows_of_x[0].shape[1] + rows_of_x[2].shape[1]
    return pl.pallas_call(
        squares_kernel,
        in_specs=[VMEM] * 8,
        out_specs=(VMEM,) * 3,
        out_shape=in_vmem(
            ((hid_b.shape[0] + 16, cols), BF16), ((TILE, rows), BF16), ((TILE, rows), BF16)
        ),
        scratch_shapes=[pltpu.VMEM((cols, rows), BF16), pltpu.VMEM((3, 8, TILE), F32)],
        compiler_params=params(20),
        cost_estimate=pl.CostEstimate(
            flops=2 * rows * width * cols, bytes_accessed=4 * rows * width, transcendentals=0
        ),
        name="squares",
    )(*rows_of_x, hid_a, hid_b)


def start_copies(copies, source, slot, arrays, hid, sems):
    for owner, i, row, at, n in copies:
        if owner == source:
            pltpu.make_async_copy(
                arrays[i].at[pl.ds(row, n), :], hid.at[slot, pl.ds(at, n), :], sems.at[slot]
            ).start()


def wait_rows(hid, slot, rows, sems):
    ref = hid.at[slot, pl.ds(0, rows), :]
    pltpu.make_async_copy(ref, ref, sems.at[slot]).wait()


def early_kernel(copies, missing, *refs):
    arrays, (xt_ref, gt_ref, pre_ref, hid, sems) = refs[:-5], refs[-5:]
    count, rows = hid.shape[0], hid.shape[1]
    m = hid.shape[2] // 3
    for k in range(count):
        start_copies(copies, k, k, arrays, hid, sems)
        if missing[k] is not None:
            at, n = missing[k]
            hid[k, at : at + n, :] = jnp.zeros((n, 3 * m), BF16)
    for k in range(count):
        wait_rows(hid, k, rows - (0 if missing[k] is None else missing[k][1]), sems)
        for i in range(3):
            lhs = gt_ref if i == 2 else xt_ref
            pre_ref[k, i] = jnp.dot(
                lhs[...], hid[k, :, i * m : (i + 1) * m], preferred_element_type=F32
            )


def early_products(copies, missing, arrays, xt, gt):
    rows = xt.shape[1]
    width = arrays[0].shape[1]
    count = len(missing)
    return pl.pallas_call(
        functools.partial(early_kernel, copies, missing),
        in_specs=[ANY] * len(arrays) + [VMEM] * 2,
        out_specs=VMEM,
        out_shape=in_vmem(((count, 3, TILE, width // 3), F32))[0],
        scratch_shapes=[
            pltpu.VMEM((count, rows, width), BF16),
            pltpu.SemaphoreType.DMA((count,)),
        ],
        compiler_params=params(12),
        cost_estimate=pl.CostEstimate(
            flops=2 * rows * TILE * width * count,
            bytes_accessed=2 * rows * width * count,
            transcendentals=0,
        ),
        name="early_products",
    )(*arrays, xt, gt)


def final_kernel(entries, plan, sums, *refs):
    arrays, refs = refs[:-6], refs[-6:]
    pre_ref, xt_ref, gt_ref, out_ref, stage, out_sems = refs
    m = stage.shape[3]
    pieces = sum(arrays[i][row : row + 16, 0:128].astype(F32) for i, row in sums)
    factors = []
    for i in range(3):
        total = jnp.sum(pieces[3 * i : 3 * i + 3, :], axis=0, keepdims=True)
        factors.append(lax.rsqrt(total[:, 0:1] / entries + EPSILON))

    def store(slot, source):
        at = position(source // 4, (0, 3, 1, 2)[source % 4])
        at = pl.ds(pl.multiple_of(at * m, m), m)
        return pltpu.make_async_copy(stage.at[slot], out_ref.at[:, :, at], out_sems.at[slot])

    slots = stage.shape[0]
    for step, (source, early, at, parts) in enumerate(plan):
        slot = step % slots
        if step >= slots:
            store(slot, plan[step - slots][0]).wait()
        for i in range(3):
            lhs = gt_ref if i == 2 else xt_ref
            grads = None if early is None else pre_ref[early, i]
            if parts:
                rows = [arrays[k][row : row + n, i * m : (i + 1) * m] for k, row, n in parts]
                rows = rows[0] if len(rows) == 1 else jnp.concatenate(rows, axis=0)
                more = jnp.dot(
                    lhs[:, at : at + rows.shape[0]], rows, preferred_element_type=F32
                )
                grads = more if grads is None else grads + more
            stage[slot, i] = (grads * factors[i]).astype(BF16)
        store(slot, source).start()
    for step in range(len(plan) - slots, len(plan)):
        store(step % slots, plan[step][0]).wait()


def final(plan, sums, arrays, pre, xt, gt, entries):
    rows = xt.shape[1]
    width = arrays[0].shape[1]
    m = width // 3
    arrays = [pltpu.with_memory_space_constraint(t, pltpu.VMEM) for t in arrays]
    return pl.pallas_call(
        functools.partial(final_kernel, entries, plan, sums),
        in_specs=[VMEM] * (len(arrays) + 3),
        out_specs=HBM,
        out_shape=jax.ShapeDtypeStruct((3, TILE, 8 * m), BF16),
        scratch_shapes=[
            pltpu.VMEM((3, 3, TILE, m), BF16),
            pltpu.SemaphoreType.DMA((3,)),
        ],
        compiler_params=params(16),
        cost_estimate=pl.CostEstimate(
            flops=rows * TILE * width * 8,
            bytes_accessed=4 * TILE * width * 8,
            transcendentals=0,
        ),
        name="final",
    )(*arrays, pre, xt, gt)


def placed(source, array, row, group, offset, count, z, size):
    out = []
    while count:
        step = min(count, size - offset)
        out.append((source, array, row, ((group + z) % 4) * size + offset, step))
        row, count, group, offset = row + step, count - step, group + 1, 0
    merged = [out[0]]
    for item in out[1:]:
        s, a, r, at, c = merged[-1]
        if at + c == item[3]:
            merged[-1] = (s, a, r, at, c + item[4])
        else:
            merged.append(item)
    return merged


def cut(width, step):
    return tuple((at, min(step, width - at)) for at in range(0, width, step))


def body(tokens, out_grad, combine, expert_ids, expert_rank, gate_weight, up_weight, down_weight):
    width = tokens.shape[1]
    expert = ("y", "x")
    hot = lax.axis_size(expert)
    rows = hot * 2 * CAP
    n = rows // 2
    weights = (gate_weight[0], up_weight[0], down_weight[0])
    ids, comb = expert_ids.T, combine.T
    tiles = width // TILE
    sent_rest = dispatch(ids, comb, expert_rank, tokens, out_grad, EARLY, tiles - EARLY, rows)
    ranks = after(expert_rank, sent_rest)
    sent = dispatch(ids, comb, ranks, tokens, out_grad, 0, EARLY, rows)
    early = EARLY * TILE

    near = near_z(sent)
    got = lax.all_to_all(
        sent_rest.reshape(hot, 2 * CAP, width - early), expert, split_axis=0, concat_axis=0, tiled=True
    )
    block = split_rows(got, (0,))
    far = far_z(near[1], near[2], n)
    block = after(block, far)
    near = list(after(tuple(near), block))
    got = lax.all_to_all(
        pack(near, far[0], far[1], hot), expert, split_axis=0, concat_axis=0, tiled=True
    )
    whole = with_other([split_rows(got, (1, 0, 2, 3))])

    near = near_z(block)
    far = far_z(near[1], near[2], n)
    part, *x0 = acts(Rows(0, whole, "whole", (0, 1, 2, 3)), n, weights, False, 20)
    near = with_other(near)
    hid_a, xa, ga, *held = acts(
        Rows(early, near, "parts", (0, 1, 2)), n, weights, True, 20, part, 0, keep=True
    )
    far = with_other(after(tuple(far), hid_a))
    hid_b, xb, gb = acts(
        Rows(early, far, "parts", (3,)), n, held, True, 16, part, 6 * n, given=True
    )

    near_a = near_z(hid_a)
    hid_b, xt, gt = squares((*x0, xa, ga, xb, gb), hid_a, hid_b)
    half = hid_a.shape[0] // 2
    up_a, down_a = after((near_a[1], near_a[2]), hid_b)
    last = [
        hid_b,
        along(jnp.concatenate([up_a[:half], hid_b]), 1),
        along(jnp.concatenate([down_a[half:], hid_b]), 3),
        along(hid_b, 2),
    ]
    near_a = with_other([hid_a, up_a, down_a])

    size = 2 * n
    copies, missing = [], []
    for a in range(2):
        for k, z in enumerate(NEAR_Z):
            copies += placed(3 * a + k, 3 * a + k, 0, 0, 0, 3 * size, z, size)
            missing.append(((3 + z) % 4 * size, size))
    copies += placed(0, 6, 0, 3, 0, size, 0, size)
    missing[0] = None
    pre = early_products(copies, missing, near_a + [hid_b], xt, gt)

    swapped = [swap(t) for t in after(last, pre)]
    last = [last[0], swapped[0]] + last[1:] + swapped[1:]
    sums, plan = [(0, size), (1, size)], []
    for a in range(2):
        up, down, far = range(2 + 3 * a, 5 + 3 * a)
        plan.append((4 * a, 3 * a, 3 * size, [(1, 0, size)] if a else []))
        plan.append((4 * a + 1, 3 * a + 1, 2 * size, [(up, half, size)]))
        plan.append((4 * a + 2, 3 * a + 2, 0, [(down, half, size)]))
        parts = placed(0, up, 0, 0, 0, half, 2, size)
        parts += placed(0, down, 0, half // size, half % size, half, 2, size)
        parts += placed(0, far, 0, 3, 0, size, 2, size)
        parts.sort(key=lambda part: part[3])
        plan.append((4 * a + 3, None, 0, [(k, row, n) for _, k, row, _, n in parts]))
        sums += [(up, half + size), (down, half + size), (far, size)]
    plan.sort(key=lambda step: step[0] % 4)
    entries = width * weights[0].shape[1] * 8
    return final(plan, sums, last, pre, xt, gt, entries)[None]


def solution(mesh):
    fine = Mesh(mesh.devices.reshape(4, 4, 4, 2), ("y", "x", "z", "core"))
    expert, cuts = ("y", "x"), ("z", "core")
    tokens = P(expert + cuts, None)
    return jax.shard_map(
        body,
        mesh=fine,
        in_specs=(
            tokens,
            tokens,
            tokens,
            tokens,
            P(),
            P(expert, None, cuts),
            P(expert, None, cuts),
            P(expert, cuts, None),
        ),
        out_specs=P(expert, None, cuts, None),
        check_vma=False,
    )
```

```python
import functools

import jax
import jax.numpy as jnp
from jax import lax
from jax.experimental import pallas as pl
from jax.experimental.pallas import tpu as pltpu
from jax.sharding import Mesh
from jax.sharding import PartitionSpec as P

CAP = 4
ROW_BITS = 3
EPSILON = 1e-06
TILE = 896
AHEAD = 3
EARLY = 2
F32 = jnp.float32
BF16 = jnp.bfloat16
ANY = pl.BlockSpec(memory_space=pl.ANY)
HBM = pl.BlockSpec(memory_space=pltpu.HBM)
VMEM = pl.BlockSpec(memory_space=pltpu.VMEM)


def params(mib):
    return pltpu.CompilerParams(vmem_limit_bytes=mib * 1024 * 1024)


NEAR_Z = (0, 3, 1)


def in_hbm(*arrays):
    return [pltpu.with_memory_space_constraint(t, pltpu.HBM) for t in arrays]


def in_vmem(*shapes):
    return tuple(pltpu.VMEM(shape, dtype) for shape, dtype in shapes)


def iota(shape, dim):
    return lax.broadcasted_iota(jnp.int32, shape, dim)


def dispatch_kernel(first, tiles, *refs):
    small, (tok, grad, out_ref), refs = refs[:3], refs[3:6], refs[6:]
    ids_ref, comb_ref, rank_ref = refs[:3]
    both, sems = refs[3:]
    for k in range(3):
        pltpu.make_async_copy(small[k], refs[k], sems.at[tiles + k]).start()
    rows = out_ref.shape[0]
    toks = tok.shape[0]
    for j in range(tiles):
        span = pl.ds((first + j) * TILE, TILE)
        pltpu.make_async_copy(tok.at[:, span], both.at[j, pl.ds(0, toks), :], sems.at[j]).start()
        pltpu.make_async_copy(grad.at[:, span], both.at[j, pl.ds(toks, toks), :], sems.at[j]).start()
    for k in range(3):
        pltpu.make_async_copy(small[k], refs[k], sems.at[tiles + k]).wait()
    routed = rank_ref.shape[0]
    ranks = rank_ref[...].reshape(1, routed)
    expert_row = iota((rows, routed), 0) >> ROW_BITS
    ident = jnp.sum(
        jnp.where(ranks == expert_row, iota((rows, routed), 1), 0), axis=1, keepdims=True
    )
    hit = jnp.zeros((rows, toks), F32)
    comb = jnp.zeros((rows, toks), F32)
    for k in range(ids_ref.shape[0]):
        same = ids_ref[k : k + 1, :] == ident
        hit = jnp.where(same, 1.0, hit)
        comb = jnp.where(same, comb_ref[k : k + 1, :], comb)
    earlier = (iota((toks, toks), 0) < iota((toks, toks), 1)).astype(BF16)
    slot = jnp.dot(hit.astype(BF16), earlier, preferred_element_type=F32)
    row = iota((rows, toks), 0)
    want = (row & (CAP - 1)).astype(F32)
    is_grad = (row & CAP) != 0
    sel = jnp.where(slot == want, hit, 0.0)
    select = jnp.concatenate(
        [jnp.where(is_grad, 0.0, sel), jnp.where(is_grad, sel, 0.0)], axis=1
    ).astype(BF16)
    weight = jnp.sum(sel * comb, axis=1, keepdims=True)
    scale = jnp.where(is_grad[:, :1], weight, 1.0)
    for j in range(tiles):
        pltpu.make_async_copy(both.at[j], both.at[j], sems.at[j]).wait()
        picked = jnp.dot(select, both[j], preferred_element_type=F32)
        out_ref[:, j * TILE : (j + 1) * TILE] = (picked * scale).astype(BF16)


def dispatch(ids, comb, ranks, tokens, out_grad, first, tiles, rows):
    toks = tokens.shape[0]
    return pl.pallas_call(
        functools.partial(dispatch_kernel, first, tiles),
        in_specs=[HBM] * 5,
        out_specs=VMEM,
        out_shape=jax.ShapeDtypeStruct((rows, tiles * TILE), BF16),
        scratch_shapes=[
            pltpu.VMEM(ids.shape, ids.dtype),
            pltpu.VMEM(comb.shape, comb.dtype),
            pltpu.VMEM(ranks.shape, ranks.dtype),
            pltpu.VMEM((tiles, 2 * toks, TILE), BF16),
            pltpu.SemaphoreType.DMA((tiles + 3,)),
        ],
        compiler_params=params(20),
        cost_estimate=pl.CostEstimate(
            flops=tiles * 8 * toks * rows * TILE, bytes_accessed=tiles * 6 * toks * TILE, transcendentals=0
        ),
        name="dispatch",
    )(*in_hbm(ids, comb, ranks, tokens, out_grad))


def split_kernel(order, in_ref, out_ref):
    source_count, width = in_ref.shape[0], in_ref.shape[2]
    rows = source_count * 2 * CAP
    half = rows // 2
    r, c = iota((rows, rows), 0), iota((rows, rows), 1)
    group = r & (half - 1)
    source = (group & -CAP) * 2 + jnp.where(r >= half, CAP, 0) + (group & (CAP - 1))
    perm = (c == source).astype(BF16)
    for i, place in enumerate(order):
        block = in_ref[:, i * 2 * CAP : (i + 1) * 2 * CAP, :].reshape(rows, width)
        out_ref[place * rows : (place + 1) * rows, :] = jnp.dot(
            perm, block, preferred_element_type=F32
        ).astype(BF16)


def split_rows(block, order):
    rows = block.shape[0] * block.shape[1]
    return pl.pallas_call(
        functools.partial(split_kernel, order),
        in_specs=[VMEM],
        out_specs=VMEM,
        out_shape=jax.ShapeDtypeStruct((rows, block.shape[2]), BF16),
        compiler_params=params(16),
        name="split_rows",
    )(block)


def pack_kernel(*refs):
    blocks, first, second, out = refs[:-3], refs[-3], refs[-2], refs[-1]
    hot, _, width = out.shape
    per = 2 * CAP
    for i, ref in enumerate(blocks):
        out[:, i * per : (i + 1) * per, :] = ref[...].reshape(hot, per, width)
    at = len(blocks) * per
    out[: hot // 2, at:, :] = first[...].reshape(hot // 2, per, width)
    out[hot // 2 :, at:, :] = second[...].reshape(hot // 2, per, width)


def pack(blocks, first, second, hot):
    per, width = 2 * CAP, first.shape[1]
    return pl.pallas_call(
        pack_kernel,
        in_specs=[VMEM] * (len(blocks) + 2),
        out_specs=VMEM,
        out_shape=jax.ShapeDtypeStruct((hot, (len(blocks) + 1) * per, width), BF16),
        compiler_params=params(16),
        name="pack",
    )(*[pltpu.with_memory_space_constraint(t, pltpu.VMEM) for t in (*blocks, first, second)])


def shift(n, k):
    return [(i, (i + k) % n) for i in range(n)]


def along(x, k):
    return lax.ppermute(x, "z", shift(4, k))


def swap(x):
    return lax.ppermute(x, "core", shift(2, 1))


def after(x, dep):
    return lax.optimization_barrier((x, dep))[0]


def near_z(block):
    return [block, along(block, 1), along(block, 3)]


def far_z(up, down, half):
    return [along(up[:half], 1), along(down[half:], 3)]


def with_other(mine):
    return list(mine) + [swap(t) for t in mine]


def position(dc, dz):
    z = lax.rem(lax.axis_index("z") + dz, 4)
    return z * 2 + lax.rem(lax.axis_index("core") + dc, 2)


class Rows:
    def __init__(self, first, arrays, kind, groups):
        self.first, self.arrays, self.kind, self.groups = first, arrays, kind, groups
        self.width = arrays[0].shape[1]

    def pinned(self):
        count = len(self.arrays) // 2 if self.kind == "parts" and self.groups[0] == 0 else 0
        return in_hbm(*self.arrays[:count]) + list(self.arrays[count:])

    def sources(self, refs, a, n):
        refs = refs[a * len(refs) // 2 : (a + 1) * len(refs) // 2]
        out = []
        for group in self.groups:
            if self.kind == "whole":
                out.append((group, refs[0], 2 * n * group, refs[0], 2 * n * group + n))
            elif group < 3:
                ref = refs[(1, 0, 2)[group]]
                out.append((group, ref, 0, ref, n))
            else:
                out.append((group, refs[-2], 0, refs[-1], 0))
        return out

    def start(self, refs, x_s, g_s, column, width, x_sem, g_sem):
        span = pl.ds(column, width)
        n = x_s.shape[0] // (2 * len(self.groups))
        core = lax.axis_index("core")
        for a in range(2):
            here = core if a == 0 else 1 - core
            for group, x, x_row, g, g_row in self.sources(refs, a, n):
                at = pl.multiple_of((group - self.groups[0]) * 2 * n + here * n, n)
                at = pl.ds(at, n)
                pltpu.make_async_copy(x.at[pl.ds(x_row, n), span], x_s.at[at, :], x_sem).start()
                pltpu.make_async_copy(g.at[pl.ds(g_row, n), span], g_s.at[at, :], g_sem).start()


def acts_kernel(rows_of, skip, last, keep, given, *refs):
    blocks, refs = refs[: len(rows_of.arrays)], refs[len(rows_of.arrays) :]
    weights, refs = refs[:3], refs[3:]
    if skip is not None:
        before, refs = refs[0], refs[1:]
    out_ref, x_s, g_s = refs[:3]
    refs = refs[3:]
    if given:
        held = weights
    else:
        held, refs = refs[:3], refs[3:]
    sems, acc_sem = refs[:2]
    acc = refs[2] if last else out_ref
    rows = acc.shape[1]
    count = rows_of.width // TILE
    if skip is not None:
        pltpu.make_async_copy(before.at[:, pl.ds(skip, rows), :], acc, acc_sem).start()

    def views(j):
        span = pl.ds(j * TILE, TILE)
        return (
            x_s.at[:, span], g_s.at[:, span], held[0].at[span, :], held[1].at[span, :], held[2].at[:, span]
        )

    def start(j):
        x, g, wg, wu, wd = views(j)
        span = pl.ds(rows_of.first + j * TILE, TILE)
        if not given:
            pltpu.make_async_copy(weights[0].at[span, :], wg, sems.at[2, j]).start()
            pltpu.make_async_copy(weights[1].at[span, :], wu, sems.at[3, j]).start()
        rows_of.start(blocks, x, g, j * TILE, TILE, sems.at[0, j], sems.at[1, j])
        if not given:
            pltpu.make_async_copy(weights[2].at[:, span], wd, sems.at[4, j]).start()

    for j in range(min(AHEAD, count)):
        start(j)
    if skip is not None:
        pltpu.make_async_copy(acc, acc, acc_sem).wait()
    for j in range(count):
        x, g, wg, wu, wd = views(j)
        for k, ref in enumerate((x, g) if given else (x, g, wg, wu, wd)):
            pltpu.make_async_copy(ref, ref, sems.at[k, j]).wait()
        if j + AHEAD < count:
            start(j + AHEAD)
        new = (
            jnp.dot(x[...], wg[...], preferred_element_type=F32),
            jnp.dot(x[...], wu[...], preferred_element_type=F32),
            lax.dot_general(
                g[...], wd[...], (((1,), (1,)), ((), ())), preferred_element_type=F32
            ),
        )
        for k in range(3):
            if j == 0 and skip is None:
                acc[k] = new[k]
            else:
                acc[k] += new[k]

    if last:
        m = acc.shape[2]
        step = 64

        @pl.loop(0, rows // step)
        def _(i):
            at = pl.ds(pl.multiple_of(i * step, step), step)
            gate, up, act = acc[0, at, :], acc[1, at, :], acc[2, at, :]
            sig = jax.nn.sigmoid(gate)
            out_ref[at, 0:m] = (act * up * sig * (1.0 + gate * (1.0 - sig))).astype(BF16)
            out_ref[at, m : 2 * m] = (act * gate * sig).astype(BF16)
            out_ref[at, 2 * m : 3 * m] = (gate * sig * up).astype(BF16)


def acts(rows_of, n, weights, last, mib, before=None, skip=None, keep=False, given=False):
    m = weights[2].shape[0]
    rows = 2 * n * len(rows_of.groups)
    width = rows_of.width
    out = ((rows, 3 * m), BF16) if last else ((3, rows, m), F32)
    outs = [out, ((rows, width), BF16), ((rows, width), BF16)]
    held = [((width, m), BF16), ((width, m), BF16), ((m, width), BF16)]
    scratch = []
    if keep:
        outs += held
    elif not given:
        scratch += [pltpu.VMEM(*shape) for shape in held]
    scratch += [pltpu.SemaphoreType.DMA((5, width // TILE)), pltpu.SemaphoreType.DMA(())]
    if last:
        scratch.append(pltpu.VMEM((3, rows, m), F32))
    extra = [] if before is None else [before]
    return pl.pallas_call(
        functools.partial(acts_kernel, rows_of, skip, last, keep, given),
        in_specs=[ANY] * len(rows_of.arrays) + [VMEM if given else HBM] * 3 + [VMEM] * len(extra),
        out_specs=(VMEM,) * len(outs),
        out_shape=in_vmem(*outs),
        scratch_shapes=scratch,
        compiler_params=params(mib),
        cost_estimate=pl.CostEstimate(
            flops=6 * rows * width * m,
            bytes_accessed=4 * rows * width + 6 * m * width,
            transcendentals=0,
        ),
        name="acts",
    )(*rows_of.pinned(), *(weights if given else in_hbm(*weights)), *extra)


def squares_kernel(x0, g0, xa, ga, xb, gb, hid_a, hid_b, last_ref, xt_ref, gt_ref, hid_t, parts):
    m = hid_a.shape[1] // 3
    rows_a = hid_a.shape[0]
    hid_t[:, :rows_a] = hid_a[...].T
    hid_t[:, rows_a:] = hid_b[...].T
    parts[...] = jnp.zeros_like(parts)
    mine = position(0, 0)

    def tile(j, x, g):
        @pl.when(j == mine)
        def _():
            xt_ref[...] = x.T
            gt_ref[...] = g.T

        both = jnp.dot(hid_t[: 2 * m, :], x, preferred_element_type=F32)
        down = jnp.dot(hid_t[2 * m :, :], g, preferred_element_type=F32)
        for i, grads in enumerate((both[:m], both[m:], down)):
            parts[i] += jnp.sum((grads * grads).reshape(m // 8, 8, TILE), axis=0)

    early = x0.shape[1] // TILE

    @pl.loop(0, early)
    def _(j):
        span = pl.ds(pl.multiple_of(j * TILE, TILE), TILE)
        tile(j, x0[:, span], g0[:, span])

    @pl.loop(0, xa.shape[1] // TILE)
    def _(j):
        span = pl.ds(pl.multiple_of(j * TILE, TILE), TILE)
        x = jnp.concatenate([xa[:, span], xb[:, span]], axis=0)
        g = jnp.concatenate([ga[:, span], gb[:, span]], axis=0)
        tile(j + early, x, g)

    rows_b = hid_b.shape[0]
    last_ref[:rows_b, :] = hid_b[...]
    row = iota((16, last_ref.shape[1]), 0)
    coded = jnp.zeros(row.shape, F32)
    for i in range(3):
        rest = jnp.broadcast_to(jnp.sum(parts[i], keepdims=True), row.shape)
        for k in range(3):
            piece = rest.astype(BF16).astype(F32)
            coded = jnp.where(row == 3 * i + k, piece, coded)
            rest = rest - piece
    last_ref[rows_b:, :] = coded.astype(BF16)


def squares(rows_of_x, hid_a, hid_b):
    rows = hid_a.shape[0] + hid_b.shape[0]
    cols = hid_a.shape[1]
    width = rows_of_x[0].shape[1] + rows_of_x[2].shape[1]
    return pl.pallas_call(
        squares_kernel,
        in_specs=[VMEM] * 8,
        out_specs=(VMEM,) * 3,
        out_shape=in_vmem(
            ((hid_b.shape[0] + 16, cols), BF16), ((TILE, rows), BF16), ((TILE, rows), BF16)
        ),
        scratch_shapes=[pltpu.VMEM((cols, rows), BF16), pltpu.VMEM((3, 8, TILE), F32)],
        compiler_params=params(20),
        cost_estimate=pl.CostEstimate(
            flops=2 * rows * width * cols, bytes_accessed=4 * rows * width, transcendentals=0
        ),
        name="squares",
    )(*rows_of_x, hid_a, hid_b)


def start_copies(copies, source, slot, arrays, hid, sems):
    for owner, i, row, at, n in copies:
        if owner == source:
            pltpu.make_async_copy(
                arrays[i].at[pl.ds(row, n), :], hid.at[slot, pl.ds(at, n), :], sems.at[slot]
            ).start()


def wait_rows(hid, slot, rows, sems):
    ref = hid.at[slot, pl.ds(0, rows), :]
    pltpu.make_async_copy(ref, ref, sems.at[slot]).wait()


def early_kernel(copies, missing, *refs):
    arrays, (xt_ref, gt_ref, pre_ref, hid, sems) = refs[:-5], refs[-5:]
    count, rows = hid.shape[0], hid.shape[1]
    m = hid.shape[2] // 3
    for k in range(count):
        start_copies(copies, k, k, arrays, hid, sems)
        if missing[k] is not None:
            at, n = missing[k]
            hid[k, at : at + n, :] = jnp.zeros((n, 3 * m), BF16)
    for k in range(count):
        wait_rows(hid, k, rows - (0 if missing[k] is None else missing[k][1]), sems)
        for i in range(3):
            lhs = gt_ref if i == 2 else xt_ref
            pre_ref[k, i] = jnp.dot(
                lhs[...], hid[k, :, i * m : (i + 1) * m], preferred_element_type=F32
            )


def early_products(copies, missing, arrays, xt, gt):
    rows = xt.shape[1]
    width = arrays[0].shape[1]
    count = len(missing)
    return pl.pallas_call(
        functools.partial(early_kernel, copies, missing),
        in_specs=[ANY] * len(arrays) + [VMEM] * 2,
        out_specs=VMEM,
        out_shape=in_vmem(((count, 3, TILE, width // 3), F32))[0],
        scratch_shapes=[
            pltpu.VMEM((count, rows, width), BF16),
            pltpu.SemaphoreType.DMA((count,)),
        ],
        compiler_params=params(12),
        cost_estimate=pl.CostEstimate(
            flops=2 * rows * TILE * width * count,
            bytes_accessed=2 * rows * width * count,
            transcendentals=0,
        ),
        name="early_products",
    )(*arrays, xt, gt)


def final_kernel(entries, plan, sums, *refs):
    arrays, refs = refs[:-6], refs[-6:]
    pre_ref, xt_ref, gt_ref, out_ref, stage, out_sems = refs
    m = stage.shape[3]
    pieces = sum(arrays[i][row : row + 16, 0:128].astype(F32) for i, row in sums)
    factors = []
    for i in range(3):
        total = jnp.sum(pieces[3 * i : 3 * i + 3, :], axis=0, keepdims=True)
        factors.append(lax.rsqrt(total[:, 0:1] / entries + EPSILON))

    def store(slot, source):
        at = position(source // 4, (0, 3, 1, 2)[source % 4])
        at = pl.ds(pl.multiple_of(at * m, m), m)
        return pltpu.make_async_copy(stage.at[slot], out_ref.at[:, :, at], out_sems.at[slot])

    slots = stage.shape[0]
    for step, (source, early, at, parts) in enumerate(plan):
        slot = step % slots
        if step >= slots:
            store(slot, plan[step - slots][0]).wait()
        for i in range(3):
            lhs = gt_ref if i == 2 else xt_ref
            grads = None if early is None else pre_ref[early, i]
            if parts:
                rows = [arrays[k][row : row + n, i * m : (i + 1) * m] for k, row, n in parts]
                rows = rows[0] if len(rows) == 1 else jnp.concatenate(rows, axis=0)
                more = jnp.dot(
                    lhs[:, at : at + rows.shape[0]], rows, preferred_element_type=F32
                )
                grads = more if grads is None else grads + more
            stage[slot, i] = (grads * factors[i]).astype(BF16)
        store(slot, source).start()
    for step in range(len(plan) - slots, len(plan)):
        store(step % slots, plan[step][0]).wait()


def final(plan, sums, arrays, pre, xt, gt, entries):
    rows = xt.shape[1]
    width = arrays[0].shape[1]
    m = width // 3
    arrays = [pltpu.with_memory_space_constraint(t, pltpu.VMEM) for t in arrays]
    return pl.pallas_call(
        functools.partial(final_kernel, entries, plan, sums),
        in_specs=[VMEM] * (len(arrays) + 3),
        out_specs=HBM,
        out_shape=jax.ShapeDtypeStruct((3, TILE, 8 * m), BF16),
        scratch_shapes=[
            pltpu.VMEM((3, 3, TILE, m), BF16),
            pltpu.SemaphoreType.DMA((3,)),
        ],
        compiler_params=params(16),
        cost_estimate=pl.CostEstimate(
            flops=rows * TILE * width * 8,
            bytes_accessed=4 * TILE * width * 8,
            transcendentals=0,
        ),
        name="final",
    )(*arrays, pre, xt, gt)


def placed(source, array, row, group, offset, count, z, size):
    out = []
    while count:
        step = min(count, size - offset)
        out.append((source, array, row, ((group + z) % 4) * size + offset, step))
        row, count, group, offset = row + step, count - step, group + 1, 0
    merged = [out[0]]
    for item in out[1:]:
        s, a, r, at, c = merged[-1]
        if at + c == item[3]:
            merged[-1] = (s, a, r, at, c + item[4])
        else:
            merged.append(item)
    return merged


def cut(width, step):
    return tuple((at, min(step, width - at)) for at in range(0, width, step))


def body(tokens, out_grad, combine, expert_ids, expert_rank, gate_weight, up_weight, down_weight):
    width = tokens.shape[1]
    expert = ("y", "x")
    hot = lax.axis_size(expert)
    rows = hot * 2 * CAP
    n = rows // 2
    weights = (gate_weight[0], up_weight[0], down_weight[0])
    ids, comb = expert_ids.T, combine.T
    tiles = width // TILE
    sent_rest = dispatch(ids, comb, expert_rank, tokens, out_grad, EARLY, tiles - EARLY, rows)
    ranks = after(expert_rank, sent_rest)
    sent = dispatch(ids, comb, ranks, tokens, out_grad, 0, EARLY, rows)
    early = EARLY * TILE

    near = near_z(sent)
    got = lax.all_to_all(
        sent_rest.reshape(hot, 2 * CAP, width - early), expert, split_axis=0, concat_axis=0, tiled=True
    )
    block = split_rows(got, (0,))
    far = far_z(near[1], near[2], n)
    block = after(block, far)
    near = list(after(tuple(near), block))
    got = lax.all_to_all(
        pack(near, far[0], far[1], hot), expert, split_axis=0, concat_axis=0, tiled=True
    )
    whole = with_other([split_rows(got, (1, 0, 2, 3))])

    near = near_z(block)
    far = far_z(near[1], near[2], n)
    part, *x0 = acts(Rows(0, whole, "whole", (0, 1, 2, 3)), n, weights, False, 20)
    near = with_other(near)
    hid_a, xa, ga, *held = acts(
        Rows(early, near, "parts", (0, 1, 2)), n, weights, True, 20, part, 0, keep=True
    )
    far = with_other(after(tuple(far), hid_a))
    hid_b, xb, gb = acts(
        Rows(early, far, "parts", (3,)), n, held, True, 16, part, 6 * n, given=True
    )

    near_a = near_z(hid_a)
    hid_b, xt, gt = squares((*x0, xa, ga, xb, gb), hid_a, hid_b)
    half = hid_a.shape[0] // 2
    up_a, down_a = after((near_a[1], near_a[2]), hid_b)
    last = [
        hid_b,
        along(jnp.concatenate([up_a[:half], hid_b]), 1),
        along(jnp.concatenate([down_a[half:], hid_b]), 3),
        along(hid_b, 2),
    ]
    near_a = with_other([hid_a, up_a, down_a])

    size = 2 * n
    copies, missing = [], []
    for a in range(2):
        for k, z in enumerate(NEAR_Z):
            copies += placed(3 * a + k, 3 * a + k, 0, 0, 0, 3 * size, z, size)
            missing.append(((3 + z) % 4 * size, size))
    copies += placed(0, 6, 0, 3, 0, size, 0, size)
    missing[0] = None
    pre = early_products(copies, missing, near_a + [hid_b], xt, gt)

    swapped = [swap(t) for t in after(last, pre)]
    last = [last[0], swapped[0]] + last[1:] + swapped[1:]
    sums, plan = [(0, size), (1, size)], []
    for a in range(2):
        up, down, far = range(2 + 3 * a, 5 + 3 * a)
        plan.append((4 * a, 3 * a, 3 * size, [(1, 0, size)] if a else []))
        plan.append((4 * a + 1, 3 * a + 1, 2 * size, [(up, half, size)]))
        plan.append((4 * a + 2, 3 * a + 2, 0, [(down, half, size)]))
        parts = placed(0, up, 0, 0, 0, half, 2, size)
        parts += placed(0, down, 0, half // size, half % size, half, 2, size)
        parts += placed(0, far, 0, 3, 0, size, 2, size)
        parts.sort(key=lambda part: part[3])
        plan.append((4 * a + 3, None, 0, [(k, row, n) for _, k, row, _, n in parts]))
        sums += [(up, half + size), (down, half + size), (far, size)]
    plan.sort(key=lambda step: step[0] % 4)
    entries = width * weights[0].shape[1] * 8
    return final(plan, sums, last, pre, xt, gt, entries)[None]


def solution(mesh):
    fine = Mesh(mesh.devices.reshape(4, 4, 4, 2), ("y", "x", "z", "core"))
    expert, cuts = ("y", "x"), ("z", "core")
    tokens = P(expert + cuts, None)
    return jax.shard_map(
        body,
        mesh=fine,
        in_specs=(
            tokens,
            tokens,
            tokens,
            tokens,
            P(),
            P(expert, None, cuts),
            P(expert, None, cuts),
            P(expert, cuts, None),
        ),
        out_specs=P(expert, None, cuts, None),
        check_vma=False,
    )
```
